512 devices in a mesh: slab: 64 (over y, z), pencil: 8 (over x, core).
Axes of the slice: x: 4, y: 4, z: 16, core: 2. Of those that a mesh axis runs over, the one named last changes fastest.
Arguments:
- cell_x: int32 [2097152], P(('slab', 'pencil')), may hold values from 0 to 31
- cell_y: int32 [2097152], P(('slab', 'pencil')), may hold values from 0 to 7
- cell_z: int32 [2097152], P(('slab', 'pencil')), may hold values from 0 to 127
- offsets: float32 [3, 2097152], P(None, ('slab', 'pencil')), may hold values from 0 to 1
- radius_bin: int32 [2097152], P(('slab', 'pencil')), may hold values from 0 to 5
- masses: float32 [2097152], P(('slab', 'pencil')), may hold values from 4 to 64
- slab_dest: int32 [2097152], P(('slab', 'pencil')), may hold values from 0 to 63, as said below
- live_counts: int32 [512], P(('slab', 'pencil')), may hold values from 2048 to 4096, as said below
Outputs:
- spectrum: float32 [2, 2048, 64, 128], P(None, 'slab', 'pencil')
The draws below stay inside these ranges and needn't reach their ends.
Inputs may be any that keep to these rules, and one draw needn't show every extreme that they name: `slab_dest`: among the 4096 rows of one device no slab is named more than 128 times, and one slab is named exactly 128 times by the rows of every device. Rows 0 to live_counts[b] - 1 of device b hold live particles; some device has all 4096 rows live.
All inputs are finite; a program needn't handle non-finite values.
Results may differ from the reference program's by a relative error of at most 0.003.
Values sent between devices are 32-bit elements; how exact they have to be, the bound alone decides.
No kernel may reach another device: no remote copies, remote signals or barrier semaphores. Data moves between devices by JAX's collectives and lax.ppermute only.
A program may use at most 64 MiB of HBM per device.

```python
import math
import jax
import jax.numpy as jnp
import numpy as np
from jax import lax

NX = 2048
GHOST = 3
NBIN = 6
CY = 8
NZ = 128
P_DEV = 4096
CX = 32
NY = 64
CAP = 128
PARTICLES = 2097152
N_SLAB = 64
N_PENCIL = 8
DEVICES = 512


def draw_slab_dest(key, part):
    slab_count = 2 * P_DEV // CAP
    hot_key, other_key = jax.random.split(key)
    hot_slab = jax.random.randint(hot_key, (), 0, slab_count)

    def one_block(block_key):
        level_key, jitter_key, shuffle_key = jax.random.split(block_key, 3)
        levels = jax.random.randint(level_key, (slab_count, 1), 0, 8)
        levels = jnp.where(jnp.arange(slab_count)[:, None] == hot_slab, 8, levels)
        jitter = jax.random.randint(jitter_key, (slab_count, CAP), 0, 1 << 20)
        scores = (levels * (1 << 20) + jitter).reshape(-1)
        ranked = jnp.argsort(-scores, stable=True)
        chosen = ranked[:P_DEV] // CAP
        return jax.random.permutation(shuffle_key, chosen).astype(jnp.int32)
    block_keys = jax.random.split(other_key, DEVICES)
    return jax.vmap(one_block)(block_keys).reshape(-1).astype(jnp.int32)


def draw_live_counts(key, part):
    count_key, full_key = jax.random.split(key)
    counts = jax.random.randint(count_key, (DEVICES,), P_DEV // 2, P_DEV + 1)
    full_device = jax.random.randint(full_key, (), 0, DEVICES)
    return jnp.where(jnp.arange(DEVICES) == full_device, P_DEV, counts).astype(jnp.int32)


def with_ends(values, rng, low, high):
    spot = [jax.random.randint(jax.random.fold_in(rng, axis), (), 0, length) for axis, length in enumerate(values.shape)]
    main_axis = values.shape.index(max(values.shape))
    next_to = spot[:main_axis] + [(spot[main_axis] + 1) % values.shape[main_axis]] + spot[main_axis + 1:]
    return values.at[tuple(spot)].set(low).at[tuple(next_to)].set(high)


def block_levels(rng, extent, shards, least, high):
    def one(axis_at, shards_of):
        heights = jax.random.uniform(jax.random.fold_in(jax.random.fold_in(rng, 6), axis_at), (shards_of,), jnp.float32, least / len(shards), high / len(shards))
        return jnp.repeat(jnp.exp(heights), extent[axis_at] // shards_of).reshape((-1,) + (1,) * (len(extent) - axis_at - 1))

    factor_of = one(*shards[0])
    for cut in shards[1:]:
        factor_of = factor_of * one(*cut)
    return factor_of


def setup_inputs(seed: int = 0) -> dict:
    key_of = jax.random.split(jax.random.key(seed), 9)
    cell_x = with_ends(jax.random.randint(key_of[0], (PARTICLES,), 0, CX), jax.random.fold_in(key_of[0], 1), 0, CX - 1).astype(jnp.int32)
    cell_y = with_ends(jax.random.randint(key_of[1], (PARTICLES,), 0, CY), jax.random.fold_in(key_of[1], 1), 0, CY - 1).astype(jnp.int32)
    cell_z = with_ends(jax.random.randint(key_of[2], (PARTICLES,), 0, NZ), jax.random.fold_in(key_of[2], 1), 0, NZ - 1).astype(jnp.int32)
    offsets = jnp.clip(1.0 * jax.random.uniform(key_of[3], (3, PARTICLES), jnp.float32) ** block_levels(key_of[3], (3, PARTICLES), ((1, 512),), -0.2, 0.2), 0.0, 1.0)
    radius_bin = with_ends(jax.random.randint(key_of[4], (PARTICLES,), 0, NBIN), jax.random.fold_in(key_of[4], 1), 0, NBIN - 1).astype(jnp.int32)
    masses = jnp.clip(jnp.exp(math.log(64.0) - 2.7725887 * jax.random.uniform(key_of[5], (PARTICLES,), jnp.float32) ** block_levels(key_of[5], (PARTICLES,), ((0, 512),), -0.2, 0.2)), 4.0, 64.0)
    slab_dest = draw_slab_dest(jax.random.fold_in(key_of[8], 71), 0)
    live_counts = draw_live_counts(jax.random.fold_in(key_of[8], 71), 0)
    return {"cell_x": cell_x, "cell_y": cell_y, "cell_z": cell_z, "offsets": offsets, "radius_bin": radius_bin, "masses": masses, "slab_dest": slab_dest, "live_counts": live_counts}


def kernel_weights(position, radius):
    base_cell = jnp.floor(position)
    fraction = position - base_cell
    tap_offsets = jnp.arange(-GHOST, GHOST + 1).astype(position.dtype)
    scaled_gap = (tap_offsets[None, :] + 0.5 - fraction[:, None]) / radius[:, None]
    bump_values = jnp.maximum(1.0 - scaled_gap * scaled_gap, 0.0)
    bump_values = bump_values * bump_values
    weights = bump_values / lax.optimization_barrier(jnp.sum(bump_values, axis=1, keepdims=True))
    return (base_cell.astype(jnp.int32), weights)

def reversed_bits(slab_count):
    bit_count = slab_count.bit_length() - 1
    return np.array([sum(((entry_value >> bit_shift & 1) << bit_count - 1 - bit_shift for bit_shift in range(bit_count))) for entry_value in range(slab_count)], dtype=np.int64)

def reference(cell_x, cell_y, cell_z, offsets, radius_bin, masses, slab_dest, live_counts):
    particle_index = jnp.arange(PARTICLES, dtype=jnp.int32)
    source_block = particle_index // P_DEV
    is_live = particle_index % P_DEV < live_counts[source_block]
    pencil_of = source_block % N_PENCIL
    weighted = jnp.where(is_live, masses, jnp.zeros_like(masses))
    pos_first = cell_x.astype(jnp.float32) + offsets[0]
    pos_second = cell_y.astype(jnp.float32) + offsets[1]
    pos_third = cell_z.astype(jnp.float32) + offsets[2]
    radius = 1.0 + 0.5 * radius_bin.astype(jnp.float32)
    block_rows = math.gcd(PARTICLES, 8192)
    block_count = PARTICLES // block_rows
    stacked = tuple((piece.reshape(block_count, block_rows) for piece in (pos_first, pos_second, pos_third, radius, weighted, slab_dest, pencil_of)))
    tap_cells = jnp.arange(-GHOST, GHOST + 1, dtype=jnp.int32)

    def deposit(density, pieces):
        first_pos, second_pos, third_pos, radii, weight_mass, destination, pencil_ids = pieces
        base_first, kernel_first = kernel_weights(first_pos, radii)
        base_second, kernel_second = kernel_weights(second_pos, radii)
        base_third, kernel_third = kernel_weights(third_pos, radii)
        plane = (kernel_first[:, :, None] * kernel_second[:, None, :] * weight_mass[:, None, None]).astype(jnp.bfloat16)
        plane = lax.optimization_barrier(plane).astype(jnp.float32)
        depth = kernel_third.astype(jnp.bfloat16)
        depth = lax.optimization_barrier(depth).astype(jnp.float32)
        values = plane[:, :, :, None] * depth[:, None, None, :]
        index_first = (destination[:, None] * CX + base_first[:, None] + tap_cells[None, :]) % NX
        index_second = (pencil_ids[:, None] * CY + base_second[:, None] + tap_cells[None, :]) % NY
        index_third = (base_third[:, None] + tap_cells[None, :]) % NZ
        flat_index = (index_first[:, :, None, None] * NY + index_second[:, None, :, None]) * NZ + index_third[:, None, None, :]
        return (density.at[flat_index.reshape(-1)].add(values.reshape(-1)), None)
    density, trailing = lax.scan(deposit, jnp.zeros((NX * NY * NZ,), jnp.float32), stacked)
    cube = density.reshape(NX, NY, NZ)
    transform = jnp.fft.fft(cube, axis=0) / math.sqrt(NX)
    reversal = reversed_bits(N_SLAB)
    row_numbers = np.arange(NX)
    frequency_rows = row_numbers % CX * N_SLAB + reversal[row_numbers // CX]
    picked = transform[jnp.asarray(frequency_rows.astype(np.int32))]
    return jnp.stack([jnp.real(picked), jnp.imag(picked)]).astype(jnp.float32)
```

```python
import math

import jax
import jax.numpy as jnp
import numpy as np
from jax import lax
from jax.experimental import pallas as pl
from jax.experimental.pallas import tpu as pltpu
from jax.sharding import PartitionSpec as P

NX = 2048
GHOST = 3
CY = 8
NZ = 128
SLABS = 64
PLANES = 32
LANES = 128
ROWS = 32
PIECES = 13
EXT = 40
GROUPS = EXT // 8
WIDE = CY + 2 * GHOST
VMEM = 48 * 1024 * 1024


def split3(value):
    high = value.astype(jnp.bfloat16).astype(jnp.float32)
    rest = value - high
    middle = rest.astype(jnp.bfloat16).astype(jnp.float32)
    return [high, middle, rest - middle]


def bucket_kernel(
    live, cell_x, cell_y, cell_z, offsets, radius_bin, masses, dest, out,
    pieces, chosen, counts, left, right,
):
    row = lax.broadcasted_iota(jnp.int32, (ROWS, LANES), 0)
    lane = lax.broadcasted_iota(jnp.int32, (ROWS, LANES), 1)
    weighted = jnp.where(row * LANES + lane < live[0], masses[...], 0.0)
    held = (
        split3(cell_x[...].astype(jnp.float32) + offsets[0])
        + split3(cell_y[...].astype(jnp.float32) + offsets[1])
        + split3(cell_z[...].astype(jnp.float32) + offsets[2])
        + split3(weighted)
        + [1.0 + 0.5 * radius_bin[...].astype(jnp.float32)]
    )
    for number, piece in enumerate(held):
        pieces[number] = piece
    slab = lax.broadcasted_iota(jnp.int32, (SLABS, LANES), 0)
    for k in range(ROWS):
        chosen[k * SLABS : (k + 1) * SLABS] = jnp.where(
            slab == dest[k : k + 1, :], 1.0, 0.0
        ).astype(jnp.bfloat16)
    first = lax.broadcasted_iota(jnp.int32, (LANES, 2 * LANES), 0)
    second = lax.broadcasted_iota(jnp.int32, (LANES, 2 * LANES), 1)
    before = jnp.where((first < second) | (second >= LANES), 1.0, 0.0).astype(jnp.bfloat16)
    counts[...] = jnp.dot(chosen[...], before, preferred_element_type=jnp.float32)
    base = jnp.zeros((SLABS, LANES), jnp.float32)
    pair = lax.broadcasted_iota(jnp.int32, (SLABS // 2, LANES), 0)
    low = lax.broadcasted_iota(jnp.int32, (2 * LANES, LANES), 0)
    for k in range(ROWS):
        target = dest[k : k + 1, :]
        found = counts[k * SLABS : (k + 1) * SLABS, :]
        rank = jnp.sum(
            jnp.where(slab == target, found[:, :LANES] + base, 0.0), axis=0, keepdims=True
        )
        base = base + found[:, LANES:]
        slot = jnp.bitwise_and(target, 1) * LANES + rank.astype(jnp.int32)
        span = slice(k * LANES, (k + 1) * LANES)
        right[:, span] = jnp.where(low == slot, 1.0, 0.0).astype(jnp.bfloat16)
        mask = pair == jnp.right_shift(target, 1)
        for number in range(PIECES):
            left[number * ROWS : (number + 1) * ROWS, span] = jnp.where(
                mask, pieces[number, k : k + 1, :], 0.0
            ).astype(jnp.bfloat16)
    sent = lax.dot_general(
        left[...], right[...], (((1,), (1,)), ((), ())), preferred_element_type=jnp.float32
    )
    for field in range(5):
        at = 3 * field * ROWS
        value = sent[at : at + ROWS]
        if field < 4:
            value = (value + sent[at + ROWS : at + 2 * ROWS]) + sent[at + 2 * ROWS : at + 3 * ROWS]
        out[:, 0, field, :] = value[:, :LANES]
        out[:, 1, field, :] = value[:, LANES:]


def tap_sum(position, inverse):
    fraction = position - jnp.floor(position)
    total = jnp.zeros_like(position)
    for tap in range(-GHOST, GHOST + 1):
        gap = (tap + 0.5 - fraction) * inverse
        bump = jnp.maximum(1.0 - gap * gap, 0.0)
        total = total + bump * bump
    return total


def bump_of(gap):
    value = jnp.maximum(1.0 - gap * gap, 0.0)
    return value * value


BLOCK = 2


def deposit_kernel(arrived, inner, lower, upper, held, total):
    inverse = 1.0 / jnp.maximum(arrived[:, 4, :], 1.0)
    held[0] = arrived[:, 0, :]
    held[1] = arrived[:, 1, :]
    held[2] = arrived[:, 2, :]
    held[3] = inverse
    held[4] = arrived[:, 3, :] / (tap_sum(held[0], inverse) * tap_sum(held[1], inverse))
    held[5] = 1.0 / tap_sum(held[2], inverse)
    total[...] = jnp.zeros_like(total)
    wide = BLOCK * LANES
    first = lax.broadcasted_iota(jnp.int32, (EXT, wide), 0).astype(jnp.float32) + (0.5 - GHOST)
    second = lax.broadcasted_iota(jnp.int32, (16, wide), 0).astype(jnp.float32) + (0.5 - GHOST)
    third = lax.broadcasted_iota(jnp.int32, (NZ, wide), 0).astype(jnp.float32) + 0.5

    def step(index, carry):
        def row(field):
            return jnp.concatenate(
                [held[field, pl.ds(index * BLOCK + part, 1), :] for part in range(BLOCK)], axis=1
            )

        scale = row(3)
        along_first = bump_of((first - row(0)) * scale) * row(4)
        along_second = bump_of((second - row(1)) * scale)
        away = jnp.abs(third - row(2))
        away = jnp.minimum(away, NZ - away)
        depth = (bump_of(away * scale) * row(5)).astype(jnp.bfloat16)
        plane = jnp.concatenate(
            [along_first * along_second[y : y + 1, :] for y in range(WIDE)], axis=0
        ).astype(jnp.bfloat16)
        total[...] += lax.dot_general(
            plane, depth, (((1,), (1,)), ((), ())), preferred_element_type=jnp.float32
        )
        return carry

    lax.fori_loop(0, SLABS // BLOCK, step, 0, unroll=2)
    lower[...] = total[: GHOST * EXT]
    inner[...] = total[GHOST * EXT : (GHOST + CY) * EXT]
    upper[...] = total[(GHOST + CY) * EXT :]


def join_kernel(inner, from_before, from_after, out):
    for y in range(CY):
        for group in range(GROUPS):
            value = inner[y * EXT + group * 8 : y * EXT + group * 8 + 8]
            if y < GHOST:
                at = y * EXT + group * 8
                value = value + from_before[at : at + 8]
            if y >= CY - GHOST:
                at = (y - CY + GHOST) * EXT + group * 8
                value = value + from_after[at : at + 8]
            out[y * 8 : y * 8 + 8, group, :] = value


def slab_kernel(table, value, out):
    for group in range(GROUPS - 1):
        rows = value[:, group, :]
        if group == 0:
            last = value[:, GROUPS - 1, :]
            rows = rows + jnp.concatenate([last[SLABS - 1 :], last[: SLABS - 1]], axis=0)
        result = jnp.dot(
            table[group], rows, precision=lax.Precision.HIGHEST, preferred_element_type=jnp.float32
        )
        out[:, group, :] = result[:SLABS]
        out[:, GROUPS - 1 + group, :] = result[SLABS:]


def plane_kernel(table, value, out):
    for y in range(CY):
        rows = value[y * 8 : y * 8 + 8].reshape(SLABS, LANES)
        out[:, y, :] = jnp.dot(
            table[...], rows, precision=lax.Precision.HIGHEST, preferred_element_type=jnp.float32
        )


def slab_tables():
    device = np.arange(SLABS)
    frequency = np.zeros(SLABS, np.int64)
    for bit in range(6):
        frequency += (device >> bit & 1) << 5 - bit
    offset = np.arange(8)[:, None] + 8 * np.arange(4)[None, :] - GHOST
    cell = PLANES * device[None, None, None, :] + offset[:, :, None, None]
    angle = 2.0 * np.pi * (frequency[None, None, :, None] * cell % NX) / NX
    table = np.concatenate([np.cos(angle), -np.sin(angle)], axis=2)
    return (table / math.sqrt(NX)).astype(np.float32)


def plane_table():
    offset = np.arange(8)[:, None] + 8 * np.arange(4)[None, :] - GHOST
    angle = 2.0 * np.pi * (np.arange(PLANES)[:, None, None] * offset[None] % PLANES) / PLANES
    real = np.stack([np.cos(angle), np.sin(angle)], axis=2)
    imag = np.stack([-np.sin(angle), np.cos(angle)], axis=2)
    return np.stack([real, imag]).reshape(2 * PLANES, 8 * 2 * 4).astype(np.float32)


def call(kernel, out, scratch=(), specs=None, flops=0, moved=0):
    return pl.pallas_call(
        kernel,
        out_shape=out,
        **({} if specs is None else {"in_specs": specs}),
        scratch_shapes=list(scratch),
        compiler_params=pltpu.CompilerParams(vmem_limit_bytes=VMEM),
        cost_estimate=pl.CostEstimate(flops=flops, bytes_accessed=moved, transcendentals=0),
    )


def shape(*dims):
    return jax.ShapeDtypeStruct(dims, jnp.float32)


def bucket(cell_x, cell_y, cell_z, offsets, radius_bin, masses, slab_dest, live_counts):
    whole = pl.BlockSpec(memory_space=pltpu.VMEM)
    block = (ROWS, LANES)
    return call(
        bucket_kernel,
        shape(SLABS // 2, 2, 5, LANES),
        [
            pltpu.VMEM((PIECES, ROWS, LANES), jnp.float32),
            pltpu.VMEM((ROWS * SLABS, LANES), jnp.bfloat16),
            pltpu.VMEM((ROWS * SLABS, 2 * LANES), jnp.float32),
            pltpu.VMEM((PIECES * ROWS, ROWS * LANES), jnp.bfloat16),
            pltpu.VMEM((2 * LANES, ROWS * LANES), jnp.bfloat16),
        ],
        [pl.BlockSpec(memory_space=pltpu.SMEM)] + [whole] * 7,
        flops=10**9,
        moved=10**6,
    )(
        live_counts,
        cell_x.reshape(block),
        cell_y.reshape(block),
        cell_z.reshape(block),
        offsets.reshape((3,) + block),
        radius_bin.reshape(block),
        masses.reshape(block),
        slab_dest.reshape(block),
    ).reshape(SLABS, 5, LANES)


def deposit(arrived):
    return call(
        deposit_kernel,
        (shape(CY * EXT, NZ), shape(GHOST * EXT, NZ), shape(GHOST * EXT, NZ)),
        [
            pltpu.VMEM((6, SLABS, LANES), jnp.float32),
            pltpu.VMEM((WIDE * EXT, NZ), jnp.float32),
        ],
        flops=10**9,
        moved=10**6,
    )(arrived)


def exchanged(value):
    return lax.all_to_all(value, "slab", split_axis=0, concat_axis=0, tiled=True)


def local(cell_x, cell_y, cell_z, offsets, radius_bin, masses, slab_dest, live_counts):
    outgoing = bucket(
        cell_x, cell_y, cell_z, offsets, radius_bin, masses, slab_dest, live_counts
    )
    arrived = exchanged(outgoing)
    inner, lower, upper = deposit(arrived)
    count = lax.axis_size("pencil")
    up = [(i, (i + 1) % count) for i in range(count)]
    down = [(j, i) for i, j in up]
    from_before = lax.ppermute(upper, "pencil", up)
    from_after = lax.ppermute(lower, "pencil", down)
    joined = call(join_kernel, shape(SLABS, GROUPS, LANES))(inner, from_before, from_after)
    crossing = exchanged(joined)
    offset = lax.axis_index("slab") % 8
    table = lax.dynamic_index_in_dim(jnp.asarray(slab_tables()), offset, 0, keepdims=False)
    partial = call(slab_kernel, shape(SLABS, 2 * (GROUPS - 1), LANES))(table, crossing)
    back = exchanged(partial)
    final = call(plane_kernel, shape(2 * PLANES, CY, NZ))(jnp.asarray(plane_table()), back)
    return final.reshape(2, PLANES, CY, NZ)


def solution(mesh):
    in_specs = (
        P(("slab", "pencil")),
        P(("slab", "pencil")),
        P(("slab", "pencil")),
        P(None, ("slab", "pencil")),
        P(("slab", "pencil")),
        P(("slab", "pencil")),
        P(("slab", "pencil")),
        P(("slab", "pencil")),
    )
    out_specs = P(None, "slab", "pencil", None)
    return jax.shard_map(local, mesh=mesh, in_specs=in_specs, out_specs=out_specs, check_vma=False)
```

```python
import math

import jax
import jax.numpy as jnp
import numpy as np
from jax import lax
from jax.experimental import pallas as pl
from jax.experimental.pallas import tpu as pltpu
from jax.sharding import PartitionSpec as P

NX = 2048
GHOST = 3
CY = 8
NZ = 128
SLABS = 64
PLANES = 32
LANES = 128
ROWS = 32
PIECES = 13
EXT = 40
GROUPS = EXT // 8
WIDE = CY + 2 * GHOST
VMEM = 48 * 1024 * 1024


def split3(value):
    high = value.astype(jnp.bfloat16).astype(jnp.float32)
    rest = value - high
    middle = rest.astype(jnp.bfloat16).astype(jnp.float32)
    return [high, middle, rest - middle]


def bucket_kernel(live, *refs):
    sources, out, staged = refs[:7], refs[7], refs[8:15]
    shifts, pieces, chosen, counts, left, right, arrivals = refs[15:]
    copies = [
        pltpu.make_async_copy(source, place, arrivals.at[number])
        for number, (source, place) in enumerate(zip(sources, staged, strict=True))
    ]
    for copy in copies:
        copy.start()
    dest, offsets, cell_x, cell_y, cell_z, radius_bin, masses = staged
    copies[0].wait()
    slab = lax.broadcasted_iota(jnp.int32, (SLABS, LANES), 0)
    for k in range(ROWS):
        chosen[k * SLABS : (k + 1) * SLABS] = jnp.where(
            slab == dest[k : k + 1, :], 1.0, 0.0
        ).astype(jnp.bfloat16)
    first = lax.broadcasted_iota(jnp.int32, (LANES, 2 * LANES), 0)
    second = lax.broadcasted_iota(jnp.int32, (LANES, 2 * LANES), 1)
    before = jnp.where((first < second) | (second >= LANES), 1.0, 0.0).astype(jnp.bfloat16)
    counts[...] = jnp.dot(chosen[...], before, preferred_element_type=jnp.float32)
    for copy in copies[1:]:
        copy.wait()
    for axis in range(3):
        for k in range(ROWS):
            shifts[axis, k : k + 1, :] = offsets[
                axis : axis + 1, k * LANES : (k + 1) * LANES
            ]
    row = lax.broadcasted_iota(jnp.int32, (ROWS, LANES), 0)
    lane = lax.broadcasted_iota(jnp.int32, (ROWS, LANES), 1)
    weighted = jnp.where(row * LANES + lane < live[0], masses[...], 0.0)
    held = (
        split3(cell_x[...].astype(jnp.float32) + shifts[0])
        + split3(cell_y[...].astype(jnp.float32) + shifts[1])
        + split3(cell_z[...].astype(jnp.float32) + shifts[2])
        + split3(weighted)
        + [1.0 + 0.5 * radius_bin[...].astype(jnp.float32)]
    )
    for number, piece in enumerate(held):
        pieces[number] = piece
    base = jnp.zeros((SLABS, LANES), jnp.float32)
    pair = lax.broadcasted_iota(jnp.int32, (SLABS // 2, LANES), 0)
    low = lax.broadcasted_iota(jnp.int32, (2 * LANES, LANES), 0)
    for k in range(ROWS):
        target = dest[k : k + 1, :]
        found = counts[k * SLABS : (k + 1) * SLABS, :]
        rank = jnp.sum(
            jnp.where(slab == target, found[:, :LANES] + base, 0.0), axis=0, keepdims=True
        )
        base = base + found[:, LANES:]
        slot = jnp.right_shift(target, 5) * LANES + rank.astype(jnp.int32)
        span = slice(k * LANES, (k + 1) * LANES)
        right[:, span] = jnp.where(low == slot, 1.0, 0.0).astype(jnp.bfloat16)
        mask = pair == jnp.bitwise_and(target, SLABS // 2 - 1)
        for number in range(PIECES):
            left[number * ROWS : (number + 1) * ROWS, span] = jnp.where(
                mask, pieces[number, k : k + 1, :], 0.0
            ).astype(jnp.bfloat16)
    sent = lax.dot_general(
        left[...], right[...], (((1,), (1,)), ((), ())), preferred_element_type=jnp.float32
    )
    for field in range(5):
        at = 3 * field * ROWS
        value = sent[at : at + ROWS]
        if field < 4:
            value = (value + sent[at + ROWS : at + 2 * ROWS]) + sent[at + 2 * ROWS : at + 3 * ROWS]
        span = slice(field * LANES, (field + 1) * LANES)
        out[: SLABS // 2, 0, span] = value[:, :LANES]
        out[SLABS // 2 :, 0, span] = value[:, LANES:]


def tap_sum(position, inverse):
    fraction = position - jnp.floor(position)
    total = jnp.zeros_like(position)
    for tap in range(-GHOST, GHOST + 1):
        gap = (tap + 0.5 - fraction) * inverse
        bump = jnp.maximum(1.0 - gap * gap, 0.0)
        total = total + bump * bump
    return total


def bump_of(gap):
    value = jnp.maximum(1.0 - gap * gap, 0.0)
    return value * value


BLOCK = 2


def deposit_kernel(place, arrived, tables, inner, near, far, table, held, total, arrival):
    copy = pltpu.make_async_copy(tables.at[place[1]], table, arrival)
    copy.start()

    def field(number):
        return arrived[:, 0, number * LANES : (number + 1) * LANES]

    inverse = 1.0 / jnp.maximum(field(4), 1.0)
    held[0] = field(0)
    held[1] = field(1)
    held[2] = field(2)
    held[3] = inverse
    held[4] = field(3) / (tap_sum(held[0], inverse) * tap_sum(held[1], inverse))
    held[5] = 1.0 / tap_sum(held[2], inverse)
    total[...] = jnp.zeros_like(total)
    wide = BLOCK * LANES
    first = lax.broadcasted_iota(jnp.int32, (EXT, wide), 0).astype(jnp.float32) + (0.5 - GHOST)
    second = lax.broadcasted_iota(jnp.int32, (16, wide), 0).astype(jnp.float32) + (0.5 - GHOST)
    third = lax.broadcasted_iota(jnp.int32, (NZ, wide), 0).astype(jnp.float32) + 0.5

    def step(index, carry):
        def row(field):
            return jnp.concatenate(
                [held[field, pl.ds(index * BLOCK + part, 1), :] for part in range(BLOCK)], axis=1
            )

        scale = row(3)
        along_first = bump_of((first - row(0)) * scale) * row(4)
        along_second = bump_of((second - row(1)) * scale)
        away = jnp.abs(third - row(2))
        away = jnp.minimum(away, NZ - away)
        depth = (bump_of(away * scale) * row(5)).astype(jnp.bfloat16)
        plane = jnp.concatenate(
            [along_first * along_second[y : y + 1, :] for y in range(WIDE)], axis=0
        ).astype(jnp.bfloat16)
        total[...] += lax.dot_general(
            plane, depth, (((1,), (1,)), ((), ())), preferred_element_type=jnp.float32
        )
        return carry

    lax.fori_loop(0, SLABS // BLOCK, step, 0, unroll=2)
    inner[...] = total[GHOST * EXT : (GHOST + CY) * EXT]
    even = place[0] == 0
    lower = total[: GHOST * EXT]
    upper = total[(GHOST + CY) * EXT :]
    near[...] = jnp.where(even, upper, lower)
    far[...] = jnp.where(even, lower, upper)
    copy.wait()


def join_kernel(place, inner, near, far, out):
    even = place[0] == 0
    for y in range(CY):
        for group in range(GROUPS):
            value = inner[y * EXT + group * 8 : y * EXT + group * 8 + 8]
            if y < GHOST:
                at = y * EXT + group * 8
                value = value + jnp.where(even, far[at : at + 8], near[at : at + 8])
            if y >= CY - GHOST:
                at = (y - CY + GHOST) * EXT + group * 8
                value = value + jnp.where(even, near[at : at + 8], far[at : at + 8])
            out[y * 8 : y * 8 + 8, 0, group * LANES : (group + 1) * LANES] = value


def slab_kernel(table, value, out):
    for group in range(GROUPS - 1):
        rows = value[:, 0, group * LANES : (group + 1) * LANES]
        if group == 0:
            last = value[:, 0, (GROUPS - 1) * LANES :]
            rows = rows + jnp.concatenate([last[SLABS - 1 :], last[: SLABS - 1]], axis=0)
        result = jnp.dot(
            table[group], rows, precision=lax.Precision.HIGHEST, preferred_element_type=jnp.float32
        )
        out[:, group, :] = result[:SLABS]
        out[:, GROUPS - 1 + group, :] = result[SLABS:]


def plane_kernel(table, value, out):
    for y in range(CY):
        rows = value[y * 8 : y * 8 + 8].reshape(SLABS, LANES)
        out[:, y, :] = jnp.dot(
            table[...], rows, precision=lax.Precision.HIGHEST, preferred_element_type=jnp.float32
        )


def slab_tables():
    device = np.arange(SLABS)
    frequency = np.zeros(SLABS, np.int64)
    for bit in range(6):
        frequency += (device >> bit & 1) << 5 - bit
    offset = np.arange(8)[:, None] + 8 * np.arange(4)[None, :] - GHOST
    cell = PLANES * device[None, None, None, :] + offset[:, :, None, None]
    angle = 2.0 * np.pi * (frequency[None, None, :, None] * cell % NX) / NX
    table = np.concatenate([np.cos(angle), -np.sin(angle)], axis=2)
    return (table / math.sqrt(NX)).astype(np.float32)


def plane_table():
    offset = np.arange(8)[:, None] + 8 * np.arange(4)[None, :] - GHOST
    angle = 2.0 * np.pi * (np.arange(PLANES)[:, None, None] * offset[None] % PLANES) / PLANES
    real = np.stack([np.cos(angle), np.sin(angle)], axis=2)
    imag = np.stack([-np.sin(angle), np.cos(angle)], axis=2)
    return np.stack([real, imag]).reshape(2 * PLANES, 8 * 2 * 4).astype(np.float32)


def call(kernel, out, scratch=(), specs=None, flops=0, moved=0):
    return pl.pallas_call(
        kernel,
        out_shape=out,
        **({} if specs is None else {"in_specs": specs}),
        scratch_shapes=list(scratch),
        compiler_params=pltpu.CompilerParams(vmem_limit_bytes=VMEM),
        cost_estimate=pl.CostEstimate(flops=flops, bytes_accessed=moved, transcendentals=0),
    )


def shape(*dims):
    return jax.ShapeDtypeStruct(dims, jnp.float32)


def bucket(cell_x, cell_y, cell_z, offsets, radius_bin, masses, slab_dest, live_counts):
    block = (ROWS, LANES)
    sources = [slab_dest.reshape(block), offsets] + [
        value.reshape(block) for value in (cell_x, cell_y, cell_z, radius_bin, masses)
    ]
    return call(
        bucket_kernel,
        shape(SLABS, 1, 5 * LANES),
        [pltpu.VMEM(value.shape, value.dtype) for value in sources]
        + [
            pltpu.VMEM((3, ROWS, LANES), jnp.float32),
            pltpu.VMEM((PIECES, ROWS, LANES), jnp.float32),
            pltpu.VMEM((ROWS * SLABS, LANES), jnp.bfloat16),
            pltpu.VMEM((ROWS * SLABS, 2 * LANES), jnp.float32),
            pltpu.VMEM((PIECES * ROWS, ROWS * LANES), jnp.bfloat16),
            pltpu.VMEM((2 * LANES, ROWS * LANES), jnp.bfloat16),
            pltpu.SemaphoreType.DMA((7,)),
        ],
        [pl.BlockSpec(memory_space=pltpu.SMEM)] + [pl.BlockSpec(memory_space=pltpu.HBM)] * 7,
        flops=10**9,
        moved=10**6,
    )(live_counts, *sources)


def deposit(place, arrived):
    here, smem = pl.BlockSpec(memory_space=pltpu.VMEM), pl.BlockSpec(memory_space=pltpu.SMEM)
    tables = jnp.asarray(slab_tables())
    rim = shape(GHOST * EXT, NZ)
    return call(
        deposit_kernel,
        (shape(CY * EXT, NZ), rim, rim, shape(*tables.shape[1:])),
        [
            pltpu.VMEM((6, SLABS, LANES), jnp.float32),
            pltpu.VMEM((WIDE * EXT, NZ), jnp.float32),
            pltpu.SemaphoreType.DMA,
        ],
        [smem, here, pl.BlockSpec(memory_space=pltpu.HBM)],
        flops=10**9,
        moved=10**6,
    )(place, arrived, tables)


def exchanged(value):
    return lax.all_to_all(value, "slab", split_axis=0, concat_axis=0, tiled=True)


def local(cell_x, cell_y, cell_z, offsets, radius_bin, masses, slab_dest, live_counts):
    outgoing = bucket(
        cell_x, cell_y, cell_z, offsets, radius_bin, masses, slab_dest, live_counts
    )
    arrived = exchanged(outgoing)
    place = jnp.stack([lax.axis_index("pencil") % 2, lax.axis_index("slab") % 8])
    inner, near, far, table = deposit(place, arrived)
    count = lax.axis_size("pencil")
    across = [(i, (i + 1 if i % 2 else i - 1) % count) for i in range(count)]
    from_far = lax.ppermute(far, "pencil", across)
    from_near = lax.ppermute(near, "pencil", [(i, i ^ 1) for i in range(count)])
    here, smem = pl.BlockSpec(memory_space=pltpu.VMEM), pl.BlockSpec(memory_space=pltpu.SMEM)
    joined = call(
        join_kernel, shape(SLABS, 1, GROUPS * LANES), specs=[smem] + [here] * 3
    )(place, inner, from_near, from_far)
    crossing = exchanged(joined)
    partial = call(slab_kernel, shape(SLABS, 2 * (GROUPS - 1), LANES))(table, crossing)
    back = exchanged(partial)
    final = call(plane_kernel, shape(2 * PLANES, CY, NZ))(jnp.asarray(plane_table()), back)
    return final.reshape(2, PLANES, CY, NZ)


def solution(mesh):
    in_specs = (
        P(("slab", "pencil")),
        P(("slab", "pencil")),
        P(("slab", "pencil")),
        P(None, ("slab", "pencil")),
        P(("slab", "pencil")),
        P(("slab", "pencil")),
        P(("slab", "pencil")),
        P(("slab", "pencil")),
    )
    out_specs = P(None, "slab", "pencil", None)
    return jax.shard_map(local, mesh=mesh, in_specs=in_specs, out_specs=out_specs, check_vma=False)
```

```python
import math

import jax
import jax.numpy as jnp
import numpy as np
from jax import lax
from jax.experimental import pallas as pl
from jax.experimental.pallas import tpu as pltpu
from jax.sharding import PartitionSpec as P

NX = 2048
GHOST = 3
CY = 8
NZ = 128
SLABS = 64
PLANES = 32
LANES = 128
ROWS = 32
PIECES = 13
EXT = 40
GROUPS = EXT // 8
WIDE = CY + 2 * GHOST
VMEM = 40 * 1024 * 1024


def split3(value):
    high = value.astype(jnp.bfloat16).astype(jnp.float32)
    rest = value - high
    middle = rest.astype(jnp.bfloat16).astype(jnp.float32)
    return [high, middle, rest - middle]


def bucket_kernel(live, *refs):
    sources, out, staged = refs[:7], refs[7], refs[8:15]
    shifts, pieces, chosen, counts, left, right, arrivals = refs[15:]
    copies = [
        pltpu.make_async_copy(source, place, arrivals.at[number])
        for number, (source, place) in enumerate(zip(sources, staged, strict=True))
    ]
    for copy in copies:
        copy.start()
    dest, offsets, cell_x, cell_y, cell_z, radius_bin, masses = staged
    copies[0].wait()
    slab = lax.broadcasted_iota(jnp.int32, (SLABS, LANES), 0)
    for k in range(ROWS):
        chosen[k * SLABS : (k + 1) * SLABS] = jnp.where(
            slab == dest[k : k + 1, :], 1.0, 0.0
        ).astype(jnp.bfloat16)
    first = lax.broadcasted_iota(jnp.int32, (LANES, 2 * LANES), 0)
    second = lax.broadcasted_iota(jnp.int32, (LANES, 2 * LANES), 1)
    before = jnp.where((first < second) | (second >= LANES), 1.0, 0.0).astype(jnp.bfloat16)
    counts[...] = jnp.dot(chosen[...], before, preferred_element_type=jnp.float32)
    for copy in copies[1:]:
        copy.wait()
    for axis in range(3):
        for k in range(ROWS):
            shifts[axis, k : k + 1, :] = offsets[
                axis : axis + 1, k * LANES : (k + 1) * LANES
            ]
    row = lax.broadcasted_iota(jnp.int32, (ROWS, LANES), 0)
    lane = lax.broadcasted_iota(jnp.int32, (ROWS, LANES), 1)
    weighted = jnp.where(row * LANES + lane < live[0], masses[...], 0.0)
    held = (
        split3(cell_x[...].astype(jnp.float32) + shifts[0])
        + split3(cell_y[...].astype(jnp.float32) + shifts[1])
        + split3(cell_z[...].astype(jnp.float32) + shifts[2])
        + split3(weighted)
        + [1.0 + 0.5 * radius_bin[...].astype(jnp.float32)]
    )
    for number, piece in enumerate(held):
        pieces[number] = piece
    base = jnp.zeros((SLABS, LANES), jnp.float32)
    pair = lax.broadcasted_iota(jnp.int32, (SLABS // 2, LANES), 0)
    low = lax.broadcasted_iota(jnp.int32, (2 * LANES, LANES), 0)
    for k in range(ROWS):
        target = dest[k : k + 1, :]
        found = counts[k * SLABS : (k + 1) * SLABS, :]
        rank = jnp.sum(
            jnp.where(slab == target, found[:, :LANES] + base, 0.0), axis=0, keepdims=True
        )
        base = base + found[:, LANES:]
        slot = jnp.right_shift(target, 5) * LANES + rank.astype(jnp.int32)
        span = slice(k * LANES, (k + 1) * LANES)
        right[:, span] = jnp.where(low == slot, 1.0, 0.0).astype(jnp.bfloat16)
        mask = pair == jnp.bitwise_and(target, SLABS // 2 - 1)
        for number in range(PIECES):
            left[number * ROWS : (number + 1) * ROWS, span] = jnp.where(
                mask, pieces[number, k : k + 1, :], 0.0
            ).astype(jnp.bfloat16)
    sent = lax.dot_general(
        left[...], right[...], (((1,), (1,)), ((), ())), preferred_element_type=jnp.float32
    )
    for field in range(5):
        at = 3 * field * ROWS
        value = sent[at : at + ROWS]
        if field < 4:
            value = (value + sent[at + ROWS : at + 2 * ROWS]) + sent[at + 2 * ROWS : at + 3 * ROWS]
        span = slice(field * LANES, (field + 1) * LANES)
        out[: SLABS // 2, 0, span] = value[:, :LANES]
        out[SLABS // 2 :, 0, span] = value[:, LANES:]


def tap_sum(position, inverse):
    fraction = position - jnp.floor(position)
    total = jnp.zeros_like(position)
    for tap in range(-GHOST, GHOST + 1):
        gap = (tap + 0.5 - fraction) * inverse
        bump = jnp.maximum(1.0 - gap * gap, 0.0)
        total = total + bump * bump
    return total


def bump_of(gap):
    value = jnp.maximum(1.0 - gap * gap, 0.0)
    return value * value


BLOCK = 2


def deposit_kernel(arrived, tables, inner, near, far, table, held, total, arrival):
    copy = pltpu.make_async_copy(tables.at[lax.axis_index("slab") % 8], table, arrival)
    copy.start()

    def field(number):
        return arrived[:, 0, number * LANES : (number + 1) * LANES]

    inverse = 1.0 / jnp.maximum(field(4), 1.0)
    held[0] = field(0)
    held[1] = field(1)
    held[2] = field(2)
    held[3] = inverse
    held[4] = field(3) / (tap_sum(held[0], inverse) * tap_sum(held[1], inverse))
    held[5] = 1.0 / tap_sum(held[2], inverse)
    total[...] = jnp.zeros_like(total)
    wide = BLOCK * LANES
    first = lax.broadcasted_iota(jnp.int32, (EXT, wide), 0).astype(jnp.float32) + (0.5 - GHOST)
    second = lax.broadcasted_iota(jnp.int32, (16, wide), 0).astype(jnp.float32) + (0.5 - GHOST)
    third = lax.broadcasted_iota(jnp.int32, (NZ, wide), 0).astype(jnp.float32) + 0.5

    def step(index, carry):
        def row(field):
            return jnp.concatenate(
                [held[field, pl.ds(index * BLOCK + part, 1), :] for part in range(BLOCK)], axis=1
            )

        scale = row(3)
        along_first = bump_of((first - row(0)) * scale) * row(4)
        along_second = bump_of((second - row(1)) * scale)
        away = jnp.abs(third - row(2))
        away = jnp.minimum(away, NZ - away)
        depth = (bump_of(away * scale) * row(5)).astype(jnp.bfloat16)
        plane = jnp.concatenate(
            [along_first * along_second[y : y + 1, :] for y in range(WIDE)], axis=0
        ).astype(jnp.bfloat16)
        total[...] += lax.dot_general(
            plane, depth, (((1,), (1,)), ((), ())), preferred_element_type=jnp.float32
        )
        return carry

    lax.fori_loop(0, SLABS // BLOCK, step, 0, unroll=2)
    inner[...] = total[GHOST * EXT : (GHOST + CY) * EXT]
    even = lax.axis_index("pencil") % 2 == 0
    lower = total[: GHOST * EXT]
    upper = total[(GHOST + CY) * EXT :]
    near[...] = jnp.where(even, upper, lower)
    far[...] = jnp.where(even, lower, upper)
    copy.wait()


def join_kernel(inner, near, far, out):
    even = lax.axis_index("pencil") % 2 == 0
    for y in range(CY):
        for group in range(GROUPS):
            value = inner[y * EXT + group * 8 : y * EXT + group * 8 + 8]
            if y < GHOST:
                at = y * EXT + group * 8
                value = value + jnp.where(even, far[at : at + 8], near[at : at + 8])
            if y >= CY - GHOST:
                at = (y - CY + GHOST) * EXT + group * 8
                value = value + jnp.where(even, near[at : at + 8], far[at : at + 8])
            out[y * 8 : y * 8 + 8, 0, group * LANES : (group + 1) * LANES] = value


def slab_kernel(table, value, out):
    for group in range(GROUPS - 1):
        rows = value[:, 0, group * LANES : (group + 1) * LANES]
        if group == 0:
            last = value[:, 0, (GROUPS - 1) * LANES :]
            rows = rows + jnp.concatenate([last[SLABS - 1 :], last[: SLABS - 1]], axis=0)
        result = jnp.dot(
            table[group], rows, precision=lax.Precision.HIGHEST, preferred_element_type=jnp.float32
        )
        out[:, group, :] = result[:SLABS]
        out[:, GROUPS - 1 + group, :] = result[SLABS:]


def plane_kernel(table, value, out):
    for y in range(CY):
        rows = value[y * 8 : y * 8 + 8].reshape(SLABS, LANES)
        out[:, y, :] = jnp.dot(
            table[...], rows, precision=lax.Precision.HIGHEST, preferred_element_type=jnp.float32
        )


def slab_tables():
    device = np.arange(SLABS)
    frequency = np.zeros(SLABS, np.int64)
    for bit in range(6):
        frequency += (device >> bit & 1) << 5 - bit
    offset = np.arange(8)[:, None] + 8 * np.arange(4)[None, :] - GHOST
    cell = PLANES * device[None, None, None, :] + offset[:, :, None, None]
    angle = 2.0 * np.pi * (frequency[None, None, :, None] * cell % NX) / NX
    table = np.concatenate([np.cos(angle), -np.sin(angle)], axis=2)
    return (table / math.sqrt(NX)).astype(np.float32)


def plane_table():
    offset = np.arange(8)[:, None] + 8 * np.arange(4)[None, :] - GHOST
    angle = 2.0 * np.pi * (np.arange(PLANES)[:, None, None] * offset[None] % PLANES) / PLANES
    real = np.stack([np.cos(angle), np.sin(angle)], axis=2)
    imag = np.stack([-np.sin(angle), np.cos(angle)], axis=2)
    return np.stack([real, imag]).reshape(2 * PLANES, 8 * 2 * 4).astype(np.float32)


def call(kernel, out, scratch=(), specs=None, flops=0, moved=0):
    return pl.pallas_call(
        kernel,
        out_shape=out,
        **({} if specs is None else {"in_specs": specs}),
        scratch_shapes=list(scratch),
        compiler_params=pltpu.CompilerParams(vmem_limit_bytes=VMEM),
        cost_estimate=pl.CostEstimate(flops=flops, bytes_accessed=moved, transcendentals=0),
    )


def shape(*dims):
    return jax.ShapeDtypeStruct(dims, jnp.float32)


def bucket(live_counts, cell_x, cell_y, cell_z, offsets, radius_bin, masses, slab_dest):
    block = (ROWS, LANES)
    sources = [slab_dest.reshape(block), offsets] + [
        value.reshape(block) for value in (cell_x, cell_y, cell_z, radius_bin, masses)
    ]
    return call(
        bucket_kernel,
        shape(SLABS, 1, 5 * LANES),
        [pltpu.VMEM(value.shape, value.dtype) for value in sources]
        + [
            pltpu.VMEM((3, ROWS, LANES), jnp.float32),
            pltpu.VMEM((PIECES, ROWS, LANES), jnp.float32),
            pltpu.VMEM((ROWS * SLABS, LANES), jnp.bfloat16),
            pltpu.VMEM((ROWS * SLABS, 2 * LANES), jnp.float32),
            pltpu.VMEM((PIECES * ROWS, ROWS * LANES), jnp.bfloat16),
            pltpu.VMEM((2 * LANES, ROWS * LANES), jnp.bfloat16),
            pltpu.SemaphoreType.DMA((7,)),
        ],
        [pl.BlockSpec(memory_space=pltpu.SMEM)] + [pl.BlockSpec(memory_space=pltpu.HBM)] * 7,
        flops=10**9,
        moved=10**6,
    )(live_counts, *[pltpu.with_memory_space_constraint(value, pltpu.HBM) for value in sources])


def deposit(arrived):
    here = pl.BlockSpec(memory_space=pltpu.VMEM)
    tables = pltpu.with_memory_space_constraint(jnp.asarray(slab_tables()), pltpu.HBM)
    rim = shape(GHOST * EXT, NZ)
    return call(
        deposit_kernel,
        (shape(CY * EXT, NZ), rim, rim, shape(*tables.shape[1:])),
        [
            pltpu.VMEM((6, SLABS, LANES), jnp.float32),
            pltpu.VMEM((WIDE * EXT, NZ), jnp.float32),
            pltpu.SemaphoreType.DMA,
        ],
        [here, pl.BlockSpec(memory_space=pltpu.HBM)],
        flops=10**9,
        moved=10**6,
    )(arrived, tables)


def exchanged(value):
    return lax.all_to_all(value, "slab", split_axis=0, concat_axis=0, tiled=True)


def local(cell_x, cell_y, cell_z, offsets, radius_bin, masses, slab_dest, live_counts):
    outgoing = bucket(
        live_counts, cell_x, cell_y, cell_z, offsets, radius_bin, masses, slab_dest
    )
    arrived = exchanged(outgoing)
    inner, near, far, table = deposit(arrived)
    count = lax.axis_size("pencil")
    across = [(i, (i + 1 if i % 2 else i - 1) % count) for i in range(count)]
    from_far = lax.ppermute(far, "pencil", across)
    from_near = lax.ppermute(near, "pencil", [(i, i ^ 1) for i in range(count)])
    joined = call(join_kernel, shape(SLABS, 1, GROUPS * LANES))(inner, from_near, from_far)
    crossing = exchanged(joined)
    partial = call(slab_kernel, shape(SLABS, 2 * (GROUPS - 1), LANES))(table, crossing)
    back = exchanged(partial)
    final = call(plane_kernel, shape(2 * PLANES, CY, NZ))(jnp.asarray(plane_table()), back)
    return final.reshape(2, PLANES, CY, NZ)


def solution(mesh):
    in_specs = (
        P(("slab", "pencil")),
        P(("slab", "pencil")),
        P(("slab", "pencil")),
        P(None, ("slab", "pencil")),
        P(("slab", "pencil")),
        P(("slab", "pencil")),
        P(("slab", "pencil")),
        P(("slab", "pencil")),
    )
    out_specs = P(None, "slab", "pencil", None)
    return jax.shard_map(local, mesh=mesh, in_specs=in_specs, out_specs=out_specs, check_vma=False)
```

```python
import math

import jax
import jax.numpy as jnp
import numpy as np
from jax import lax
from jax.experimental import pallas as pl
from jax.experimental.pallas import tpu as pltpu
from jax.sharding import PartitionSpec as P

NX = 2048
GHOST = 3
CY = 8
NZ = 128
SLABS = 64
PLANES = 32
LANES = 128
ROWS = 32
PIECES = 13
EXT = 40
GROUPS = EXT // 8
WIDE = CY + 2 * GHOST
VMEM = 40 * 1024 * 1024


def split3(value):
    high = value.astype(jnp.bfloat16).astype(jnp.float32)
    rest = value - high
    middle = rest.astype(jnp.bfloat16).astype(jnp.float32)
    return [high, middle, rest - middle]


def bucket_kernel(live, *refs):
    sources, out, staged = refs[:7], refs[7], refs[8:15]
    shifts, pieces, chosen, counts, left, right, arrivals = refs[15:]
    copies = [
        pltpu.make_async_copy(source, place, arrivals.at[number])
        for number, (source, place) in enumerate(zip(sources, staged, strict=True))
    ]
    for copy in copies:
        copy.start()
    dest, offsets, cell_x, cell_y, cell_z, radius_bin, masses = staged
    copies[0].wait()
    slab = lax.broadcasted_iota(jnp.int32, (SLABS, LANES), 0)
    for k in range(ROWS):
        chosen[k * SLABS : (k + 1) * SLABS] = jnp.where(
            slab == dest[k : k + 1, :], 1.0, 0.0
        ).astype(jnp.bfloat16)
    first = lax.broadcasted_iota(jnp.int32, (LANES, 2 * LANES), 0)
    second = lax.broadcasted_iota(jnp.int32, (LANES, 2 * LANES), 1)
    before = jnp.where((first < second) | (second >= LANES), 1.0, 0.0).astype(jnp.bfloat16)
    counts[...] = jnp.dot(chosen[...], before, preferred_element_type=jnp.float32)
    for copy in copies[1:]:
        copy.wait()
    for axis in range(3):
        for k in range(ROWS):
            shifts[axis, k : k + 1, :] = offsets[
                axis : axis + 1, k * LANES : (k + 1) * LANES
            ]
    row = lax.broadcasted_iota(jnp.int32, (ROWS, LANES), 0)
    lane = lax.broadcasted_iota(jnp.int32, (ROWS, LANES), 1)
    weighted = jnp.where(row * LANES + lane < live[0], masses[...], 0.0)
    held = (
        split3(cell_x[...].astype(jnp.float32) + shifts[0])
        + split3(cell_y[...].astype(jnp.float32) + shifts[1])
        + split3(cell_z[...].astype(jnp.float32) + shifts[2])
        + split3(weighted)
        + [1.0 + 0.5 * radius_bin[...].astype(jnp.float32)]
    )
    for number, piece in enumerate(held):
        pieces[number] = piece
    base = jnp.zeros((SLABS, LANES), jnp.float32)
    pair = lax.broadcasted_iota(jnp.int32, (SLABS // 2, LANES), 0)
    low = lax.broadcasted_iota(jnp.int32, (2 * LANES, LANES), 0)
    for k in range(ROWS):
        target = dest[k : k + 1, :]
        found = counts[k * SLABS : (k + 1) * SLABS, :]
        rank = jnp.sum(
            jnp.where(slab == target, found[:, :LANES] + base, 0.0), axis=0, keepdims=True
        )
        base = base + found[:, LANES:]
        slot = jnp.right_shift(target, 5) * LANES + rank.astype(jnp.int32)
        span = slice(k * LANES, (k + 1) * LANES)
        right[:, span] = jnp.where(low == slot, 1.0, 0.0).astype(jnp.bfloat16)
        mask = pair == jnp.bitwise_and(target, SLABS // 2 - 1)
        for number in range(PIECES):
            left[number * ROWS : (number + 1) * ROWS, span] = jnp.where(
                mask, pieces[number, k : k + 1, :], 0.0
            ).astype(jnp.bfloat16)
    sent = lax.dot_general(
        left[...], right[...], (((1,), (1,)), ((), ())), preferred_element_type=jnp.float32
    )
    for field in range(5):
        at = 3 * field * ROWS
        value = sent[at : at + ROWS]
        if field < 4:
            value = (value + sent[at + ROWS : at + 2 * ROWS]) + sent[at + 2 * ROWS : at + 3 * ROWS]
        span = slice(field * LANES, (field + 1) * LANES)
        out[: SLABS // 2, 0, span] = value[:, :LANES]
        out[SLABS // 2 :, 0, span] = value[:, LANES:]


def tap_sum(position, inverse):
    fraction = position - jnp.floor(position)
    total = jnp.zeros_like(position)
    for tap in range(-GHOST, GHOST + 1):
        gap = (tap + 0.5 - fraction) * inverse
        bump = jnp.maximum(1.0 - gap * gap, 0.0)
        total = total + bump * bump
    return total


def bump_of(gap):
    value = jnp.maximum(1.0 - gap * gap, 0.0)
    return value * value


BLOCK = 16


def deposit_kernel(arrived, tables, inner, lower, upper, table, held, total, arrival):
    copy = pltpu.make_async_copy(tables.at[lax.axis_index("slab") % 8], table, arrival)
    copy.start()

    def field(number):
        return arrived[:, 0, number * LANES : (number + 1) * LANES]

    inverse = 1.0 / jnp.maximum(field(4), 1.0)
    held[0] = field(0)
    held[1] = field(1)
    held[2] = field(2)
    held[3] = inverse
    held[4] = field(3) / (tap_sum(held[0], inverse) * tap_sum(held[1], inverse))
    held[5] = 1.0 / tap_sum(held[2], inverse)
    total[...] = jnp.zeros_like(total)
    wide = BLOCK * LANES
    first = lax.broadcasted_iota(jnp.int32, (EXT, wide), 0).astype(jnp.float32) + (0.5 - GHOST)
    second = lax.broadcasted_iota(jnp.int32, (16, wide), 0).astype(jnp.float32) + (0.5 - GHOST)
    third = lax.broadcasted_iota(jnp.int32, (NZ, wide), 0).astype(jnp.float32) + 0.5

    def step(index, carry):
        def row(field):
            return jnp.concatenate(
                [held[field, pl.ds(index * BLOCK + part, 1), :] for part in range(BLOCK)], axis=1
            )

        scale = row(3)
        along_first = bump_of((first - row(0)) * scale) * row(4)
        along_second = bump_of((second - row(1)) * scale)
        away = jnp.abs(third - row(2))
        away = jnp.minimum(away, NZ - away)
        depth = (bump_of(away * scale) * row(5)).astype(jnp.bfloat16)
        plane = jnp.concatenate(
            [along_first * along_second[y : y + 1, :] for y in range(WIDE)], axis=0
        ).astype(jnp.bfloat16)
        total[...] += lax.dot_general(
            plane, depth, (((1,), (1,)), ((), ())), preferred_element_type=jnp.float32
        )
        return carry

    lax.fori_loop(0, SLABS // BLOCK, step, 0, unroll=2)
    inner[...] = total[GHOST * EXT : (GHOST + CY) * EXT]
    lower[...] = total[: GHOST * EXT]
    upper[...] = total[(GHOST + CY) * EXT :]
    copy.wait()


def join_kernel(inner, before, after, out):
    for y in range(CY):
        for group in range(GROUPS):
            value = inner[y * EXT + group * 8 : y * EXT + group * 8 + 8]
            if y < GHOST:
                at = y * EXT + group * 8
                value = value + before[at : at + 8]
            if y >= CY - GHOST:
                at = (y - CY + GHOST) * EXT + group * 8
                value = value + after[at : at + 8]
            out[y * 8 : y * 8 + 8, 0, group * LANES : (group + 1) * LANES] = value


def slab_kernel(table, value, out):
    for group in range(GROUPS - 1):
        rows = value[:, 0, group * LANES : (group + 1) * LANES]
        if group == 0:
            last = value[:, 0, (GROUPS - 1) * LANES :]
            rows = rows + jnp.concatenate([last[SLABS - 1 :], last[: SLABS - 1]], axis=0)
        result = jnp.dot(
            table[group], rows, precision=lax.Precision.HIGHEST, preferred_element_type=jnp.float32
        )
        out[:, group, :] = result[:SLABS]
        out[:, GROUPS - 1 + group, :] = result[SLABS:]


def plane_kernel(table, value, out, held, leaves):
    rows = jnp.concatenate(
        [value[y * 8 : y * 8 + 8].reshape(SLABS, LANES) for y in range(CY)], axis=1
    )
    copies = []
    for part in range(2):
        span = pl.ds(part * PLANES, PLANES)
        result = jnp.dot(
            table[span, :], rows, precision=lax.Precision.HIGHEST, preferred_element_type=jnp.float32
        )
        for y in range(CY):
            held[span, y, :] = result[:, y * LANES : (y + 1) * LANES]
        copies.append(pltpu.make_async_copy(held.at[span], out.at[span], leaves.at[part]))
        copies[part].start()
    for copy in copies:
        copy.wait()


def slab_tables():
    device = np.arange(SLABS)
    frequency = np.zeros(SLABS, np.int64)
    for bit in range(6):
        frequency += (device >> bit & 1) << 5 - bit
    offset = np.arange(8)[:, None] + 8 * np.arange(4)[None, :] - GHOST
    cell = PLANES * device[None, None, None, :] + offset[:, :, None, None]
    angle = 2.0 * np.pi * (frequency[None, None, :, None] * cell % NX) / NX
    table = np.concatenate([np.cos(angle), -np.sin(angle)], axis=2)
    return (table / math.sqrt(NX)).astype(np.float32)


def plane_table():
    offset = np.arange(8)[:, None] + 8 * np.arange(4)[None, :] - GHOST
    angle = 2.0 * np.pi * (np.arange(PLANES)[:, None, None] * offset[None] % PLANES) / PLANES
    real = np.stack([np.cos(angle), np.sin(angle)], axis=2)
    imag = np.stack([-np.sin(angle), np.cos(angle)], axis=2)
    return np.stack([real, imag]).reshape(2 * PLANES, 8 * 2 * 4).astype(np.float32)


def call(kernel, out, scratch=(), specs=None, leave=None, flops=0, moved=0):
    return pl.pallas_call(
        kernel,
        out_shape=out,
        **({} if specs is None else {"in_specs": specs}),
        **({} if leave is None else {"out_specs": leave}),
        scratch_shapes=list(scratch),
        compiler_params=pltpu.CompilerParams(vmem_limit_bytes=VMEM),
        cost_estimate=pl.CostEstimate(flops=flops, bytes_accessed=moved, transcendentals=0),
    )


def shape(*dims):
    return jax.ShapeDtypeStruct(dims, jnp.float32)


def bucket(live_counts, cell_x, cell_y, cell_z, offsets, radius_bin, masses, slab_dest):
    block = (ROWS, LANES)
    sources = [slab_dest.reshape(block), offsets] + [
        value.reshape(block) for value in (cell_x, cell_y, cell_z, radius_bin, masses)
    ]
    return call(
        bucket_kernel,
        shape(SLABS, 1, 5 * LANES),
        [pltpu.VMEM(value.shape, value.dtype) for value in sources]
        + [
            pltpu.VMEM((3, ROWS, LANES), jnp.float32),
            pltpu.VMEM((PIECES, ROWS, LANES), jnp.float32),
            pltpu.VMEM((ROWS * SLABS, LANES), jnp.bfloat16),
            pltpu.VMEM((ROWS * SLABS, 2 * LANES), jnp.float32),
            pltpu.VMEM((PIECES * ROWS, ROWS * LANES), jnp.bfloat16),
            pltpu.VMEM((2 * LANES, ROWS * LANES), jnp.bfloat16),
            pltpu.SemaphoreType.DMA((7,)),
        ],
        [pl.BlockSpec(memory_space=pltpu.SMEM)] + [pl.BlockSpec(memory_space=pltpu.HBM)] * 7,
        flops=10**9,
        moved=10**6,
    )(live_counts, *[pltpu.with_memory_space_constraint(value, pltpu.HBM) for value in sources])


def deposit(arrived):
    here = pl.BlockSpec(memory_space=pltpu.VMEM)
    tables = pltpu.with_memory_space_constraint(jnp.asarray(slab_tables()), pltpu.HBM)
    rim = shape(GHOST * EXT, NZ)
    return call(
        deposit_kernel,
        (shape(CY * EXT, NZ), rim, rim, shape(*tables.shape[1:])),
        [
            pltpu.VMEM((6, SLABS, LANES), jnp.float32),
            pltpu.VMEM((WIDE * EXT, NZ), jnp.float32),
            pltpu.SemaphoreType.DMA,
        ],
        [here, pl.BlockSpec(memory_space=pltpu.HBM)],
        flops=10**9,
        moved=10**6,
    )(arrived, tables)


def exchanged(value):
    return lax.all_to_all(value, "slab", split_axis=0, concat_axis=0, tiled=True)


def local(cell_x, cell_y, cell_z, offsets, radius_bin, masses, slab_dest, live_counts):
    outgoing = bucket(
        live_counts, cell_x, cell_y, cell_z, offsets, radius_bin, masses, slab_dest
    )
    arrived = exchanged(outgoing)
    inner, lower, upper, table = deposit(arrived)
    count = lax.axis_size("pencil")
    up = [(i, (i + 1) % count) for i in range(count)]
    before = lax.ppermute(upper, "pencil", up)
    after = lax.ppermute(lower, "pencil", [(j, i) for i, j in up])
    joined = call(join_kernel, shape(SLABS, 1, GROUPS * LANES))(inner, before, after)
    crossing = exchanged(joined)
    partial = call(slab_kernel, shape(SLABS, 2 * (GROUPS - 1), LANES))(table, crossing)
    back = exchanged(partial)
    final = call(
        plane_kernel,
        shape(2 * PLANES, CY, NZ),
        [pltpu.VMEM((2 * PLANES, CY, NZ), jnp.float32), pltpu.SemaphoreType.DMA((2,))],
        leave=pl.BlockSpec(memory_space=pltpu.HBM),
    )(jnp.asarray(plane_table()), back)
    return final.reshape(2, PLANES, CY, NZ)


def solution(mesh):
    in_specs = (
        P(("slab", "pencil")),
        P(("slab", "pencil")),
        P(("slab", "pencil")),
        P(None, ("slab", "pencil")),
        P(("slab", "pencil")),
        P(("slab", "pencil")),
        P(("slab", "pencil")),
        P(("slab", "pencil")),
    )
    out_specs = P(None, "slab", "pencil", None)
    return jax.shard_map(local, mesh=mesh, in_specs=in_specs, out_specs=out_specs, check_vma=False)
```

```python
import math

import jax
import jax.numpy as jnp
import numpy as np
from jax import lax
from jax.experimental import pallas as pl
from jax.experimental.pallas import tpu as pltpu
from jax.sharding import PartitionSpec as P

NX = 2048
GHOST = 3
CY = 8
NZ = 128
SLABS = 64
PLANES = 32
LANES = 128
ROWS = 32
PIECES = 13
EXT = 40
GROUPS = EXT // 8
WIDE = CY + 2 * GHOST
VMEM = 40 * 1024 * 1024


def split3(value):
    high = value.astype(jnp.bfloat16).astype(jnp.float32)
    rest = value - high
    middle = rest.astype(jnp.bfloat16).astype(jnp.float32)
    return [high, middle, rest - middle]


def bucket_kernel(live, *refs):
    sources, out, staged = refs[:7], refs[7], refs[8:15]
    shifts, pieces, chosen, counts, left, right, arrivals = refs[15:]
    copies = [
        pltpu.make_async_copy(source, place, arrivals.at[number])
        for number, (source, place) in enumerate(zip(sources, staged, strict=True))
    ]
    for copy in copies:
        copy.start()
    dest, offsets, cell_x, cell_y, cell_z, radius_bin, masses = staged
    copies[0].wait()
    slab = lax.broadcasted_iota(jnp.int32, (SLABS, LANES), 0)
    for k in range(ROWS):
        chosen[k * SLABS : (k + 1) * SLABS] = jnp.where(
            slab == dest[k : k + 1, :], 1.0, 0.0
        ).astype(jnp.bfloat16)
    first = lax.broadcasted_iota(jnp.int32, (LANES, 2 * LANES), 0)
    second = lax.broadcasted_iota(jnp.int32, (LANES, 2 * LANES), 1)
    before = jnp.where((first < second) | (second >= LANES), 1.0, 0.0).astype(jnp.bfloat16)
    counts[...] = jnp.dot(chosen[...], before, preferred_element_type=jnp.float32)
    for copy in copies[1:]:
        copy.wait()
    for axis in range(3):
        for k in range(ROWS):
            shifts[axis, k : k + 1, :] = offsets[
                axis : axis + 1, k * LANES : (k + 1) * LANES
            ]
    row = lax.broadcasted_iota(jnp.int32, (ROWS, LANES), 0)
    lane = lax.broadcasted_iota(jnp.int32, (ROWS, LANES), 1)
    weighted = jnp.where(row * LANES + lane < live[0], masses[...], 0.0)
    held = (
        split3(cell_x[...].astype(jnp.float32) + shifts[0])
        + split3(cell_y[...].astype(jnp.float32) + shifts[1])
        + split3(cell_z[...].astype(jnp.float32) + shifts[2])
        + split3(weighted)
        + [1.0 + 0.5 * radius_bin[...].astype(jnp.float32)]
    )
    for number, piece in enumerate(held):
        pieces[number] = piece
    base = jnp.zeros((SLABS, LANES), jnp.float32)
    pair = lax.broadcasted_iota(jnp.int32, (SLABS // 2, LANES), 0)
    low = lax.broadcasted_iota(jnp.int32, (2 * LANES, LANES), 0)
    for k in range(ROWS):
        target = dest[k : k + 1, :]
        found = counts[k * SLABS : (k + 1) * SLABS, :]
        rank = jnp.sum(
            jnp.where(slab == target, found[:, :LANES] + base, 0.0), axis=0, keepdims=True
        )
        base = base + found[:, LANES:]
        slot = jnp.right_shift(target, 5) * LANES + rank.astype(jnp.int32)
        span = slice(k * LANES, (k + 1) * LANES)
        right[:, span] = jnp.where(low == slot, 1.0, 0.0).astype(jnp.bfloat16)
        mask = pair == jnp.bitwise_and(target, SLABS // 2 - 1)
        for number in range(PIECES):
            left[number * ROWS : (number + 1) * ROWS, span] = jnp.where(
                mask, pieces[number, k : k + 1, :], 0.0
            ).astype(jnp.bfloat16)
    sent = lax.dot_general(
        left[...], right[...], (((1,), (1,)), ((), ())), preferred_element_type=jnp.float32
    )
    for field in range(5):
        at = 3 * field * ROWS
        value = sent[at : at + ROWS]
        if field < 4:
            value = (value + sent[at + ROWS : at + 2 * ROWS]) + sent[at + 2 * ROWS : at + 3 * ROWS]
        span = slice(field * LANES, (field + 1) * LANES)
        out[: SLABS // 2, 0, span] = value[:, :LANES]
        out[SLABS // 2 :, 0, span] = value[:, LANES:]


def tap_sum(position, inverse):
    fraction = position - jnp.floor(position)
    total = jnp.zeros_like(position)
    for tap in range(-GHOST, GHOST + 1):
        gap = (tap + 0.5 - fraction) * inverse
        bump = jnp.maximum(1.0 - gap * gap, 0.0)
        total = total + bump * bump
    return total


def bump_of(gap):
    value = jnp.maximum(1.0 - gap * gap, 0.0)
    return value * value


BLOCK = 16


def deposit_rows(arrived, held, total, wanted):
    def field(number):
        return arrived[:, 0, number * LANES : (number + 1) * LANES]

    inverse = 1.0 / jnp.maximum(field(4), 1.0)
    held[0] = field(0)
    held[1] = field(1)
    held[2] = field(2)
    held[3] = inverse
    held[4] = field(3) / (tap_sum(held[0], inverse) * tap_sum(held[1], inverse))
    held[5] = 1.0 / tap_sum(held[2], inverse)
    total[...] = jnp.zeros_like(total)
    wide = BLOCK * LANES
    first = lax.broadcasted_iota(jnp.int32, (EXT, wide), 0).astype(jnp.float32) + (0.5 - GHOST)
    second = lax.broadcasted_iota(jnp.int32, (16, wide), 0).astype(jnp.float32) + (0.5 - GHOST)
    third = lax.broadcasted_iota(jnp.int32, (NZ, wide), 0).astype(jnp.float32) + 0.5

    def step(index, carry):
        def row(field):
            return jnp.concatenate(
                [held[field, pl.ds(index * BLOCK + part, 1), :] for part in range(BLOCK)], axis=1
            )

        scale = row(3)
        along_first = bump_of((first - row(0)) * scale) * row(4)
        along_second = bump_of((second - row(1)) * scale)
        away = jnp.abs(third - row(2))
        away = jnp.minimum(away, NZ - away)
        depth = (bump_of(away * scale) * row(5)).astype(jnp.bfloat16)
        plane = jnp.concatenate(
            [along_first * along_second[y : y + 1, :] for y in wanted], axis=0
        ).astype(jnp.bfloat16)
        total[...] += lax.dot_general(
            plane, depth, (((1,), (1,)), ((), ())), preferred_element_type=jnp.float32
        )
        return carry

    lax.fori_loop(0, SLABS // BLOCK, step, 0, unroll=2)


def rim_kernel(arrived, lower, upper, held, total):
    deposit_rows(arrived, held, total, [*range(GHOST), *range(GHOST + CY, WIDE)])
    lower[...] = total[: GHOST * EXT]
    upper[...] = total[GHOST * EXT :]


def inner_kernel(arrived, tables, inner, table, held, arrival):
    copy = pltpu.make_async_copy(tables.at[lax.axis_index("slab") % 8], table, arrival)
    copy.start()
    deposit_rows(arrived, held, inner, range(GHOST, GHOST + CY))
    copy.wait()


def join_kernel(inner, before, after, out):
    for y in range(CY):
        for group in range(GROUPS):
            value = inner[y * EXT + group * 8 : y * EXT + group * 8 + 8]
            if y < GHOST:
                at = y * EXT + group * 8
                value = value + before[at : at + 8]
            if y >= CY - GHOST:
                at = (y - CY + GHOST) * EXT + group * 8
                value = value + after[at : at + 8]
            out[y * 8 : y * 8 + 8, 0, group * LANES : (group + 1) * LANES] = value


def slab_kernel(table, value, out):
    for group in range(GROUPS - 1):
        rows = value[:, 0, group * LANES : (group + 1) * LANES]
        if group == 0:
            last = value[:, 0, (GROUPS - 1) * LANES :]
            rows = rows + jnp.concatenate([last[SLABS - 1 :], last[: SLABS - 1]], axis=0)
        result = jnp.dot(
            table[group], rows, precision=lax.Precision.HIGHEST, preferred_element_type=jnp.float32
        )
        out[:, group, :] = result[:SLABS]
        out[:, GROUPS - 1 + group, :] = result[SLABS:]


def plane_kernel(table, value, out, held, leaves):
    rows = jnp.concatenate(
        [value[y * 8 : y * 8 + 8].reshape(SLABS, LANES) for y in range(CY)], axis=1
    )
    copies = []
    for part in range(2):
        span = pl.ds(part * PLANES, PLANES)
        result = jnp.dot(
            table[span, :], rows, precision=lax.Precision.HIGHEST, preferred_element_type=jnp.float32
        )
        for y in range(CY):
            held[span, y, :] = result[:, y * LANES : (y + 1) * LANES]
        copies.append(pltpu.make_async_copy(held.at[span], out.at[span], leaves.at[part]))
        copies[part].start()
    for copy in copies:
        copy.wait()


def slab_tables():
    device = np.arange(SLABS)
    frequency = np.zeros(SLABS, np.int64)
    for bit in range(6):
        frequency += (device >> bit & 1) << 5 - bit
    offset = np.arange(8)[:, None] + 8 * np.arange(4)[None, :] - GHOST
    cell = PLANES * device[None, None, None, :] + offset[:, :, None, None]
    angle = 2.0 * np.pi * (frequency[None, None, :, None] * cell % NX) / NX
    table = np.concatenate([np.cos(angle), -np.sin(angle)], axis=2)
    return (table / math.sqrt(NX)).astype(np.float32)


def plane_table():
    offset = np.arange(8)[:, None] + 8 * np.arange(4)[None, :] - GHOST
    angle = 2.0 * np.pi * (np.arange(PLANES)[:, None, None] * offset[None] % PLANES) / PLANES
    real = np.stack([np.cos(angle), np.sin(angle)], axis=2)
    imag = np.stack([-np.sin(angle), np.cos(angle)], axis=2)
    return np.stack([real, imag]).reshape(2 * PLANES, 8 * 2 * 4).astype(np.float32)


def call(kernel, out, scratch=(), specs=None, leave=None, flops=0, moved=0):
    return pl.pallas_call(
        kernel,
        out_shape=out,
        **({} if specs is None else {"in_specs": specs}),
        **({} if leave is None else {"out_specs": leave}),
        scratch_shapes=list(scratch),
        compiler_params=pltpu.CompilerParams(vmem_limit_bytes=VMEM),
        cost_estimate=pl.CostEstimate(flops=flops, bytes_accessed=moved, transcendentals=0),
    )


def shape(*dims):
    return jax.ShapeDtypeStruct(dims, jnp.float32)


def bucket(live_counts, cell_x, cell_y, cell_z, offsets, radius_bin, masses, slab_dest):
    block = (ROWS, LANES)
    sources = [slab_dest.reshape(block), offsets] + [
        value.reshape(block) for value in (cell_x, cell_y, cell_z, radius_bin, masses)
    ]
    return call(
        bucket_kernel,
        shape(SLABS, 1, 5 * LANES),
        [pltpu.VMEM(value.shape, value.dtype) for value in sources]
        + [
            pltpu.VMEM((3, ROWS, LANES), jnp.float32),
            pltpu.VMEM((PIECES, ROWS, LANES), jnp.float32),
            pltpu.VMEM((ROWS * SLABS, LANES), jnp.bfloat16),
            pltpu.VMEM((ROWS * SLABS, 2 * LANES), jnp.float32),
            pltpu.VMEM((PIECES * ROWS, ROWS * LANES), jnp.bfloat16),
            pltpu.VMEM((2 * LANES, ROWS * LANES), jnp.bfloat16),
            pltpu.SemaphoreType.DMA((7,)),
        ],
        [pl.BlockSpec(memory_space=pltpu.SMEM)] + [pl.BlockSpec(memory_space=pltpu.HBM)] * 7,
        flops=10**9,
        moved=10**6,
    )(live_counts, *[pltpu.with_memory_space_constraint(value, pltpu.HBM) for value in sources])


HELD = pltpu.VMEM((6, SLABS, LANES), jnp.float32)


def deposit_rims(arrived):
    rim = shape(GHOST * EXT, NZ)
    scratch = [HELD, pltpu.VMEM((2 * GHOST * EXT, NZ), jnp.float32)]
    return call(rim_kernel, (rim, rim), scratch, flops=5 * 10**8, moved=10**6)(arrived)


def deposit_inner(arrived):
    tables = pltpu.with_memory_space_constraint(jnp.asarray(slab_tables()), pltpu.HBM)
    return call(
        inner_kernel,
        (shape(CY * EXT, NZ), shape(*tables.shape[1:])),
        [HELD, pltpu.SemaphoreType.DMA],
        [pl.BlockSpec(memory_space=pltpu.VMEM), pl.BlockSpec(memory_space=pltpu.HBM)],
        flops=10**9,
        moved=10**6,
    )(arrived, tables)


def exchanged(value):
    return lax.all_to_all(value, "slab", split_axis=0, concat_axis=0, tiled=True)


def local(cell_x, cell_y, cell_z, offsets, radius_bin, masses, slab_dest, live_counts):
    outgoing = bucket(
        live_counts, cell_x, cell_y, cell_z, offsets, radius_bin, masses, slab_dest
    )
    arrived = exchanged(outgoing)
    lower, upper = deposit_rims(arrived)
    count = lax.axis_size("pencil")
    up = [(i, (i + 1) % count) for i in range(count)]
    before = lax.ppermute(upper, "pencil", up)
    after = lax.ppermute(lower, "pencil", [(j, i) for i, j in up])
    inner, table = deposit_inner(arrived)
    joined = call(join_kernel, shape(SLABS, 1, GROUPS * LANES))(inner, before, after)
    crossing = exchanged(joined)
    partial = call(slab_kernel, shape(SLABS, 2 * (GROUPS - 1), LANES))(table, crossing)
    back = exchanged(partial)
    final = call(
        plane_kernel,
        shape(2 * PLANES, CY, NZ),
        [pltpu.VMEM((2 * PLANES, CY, NZ), jnp.float32), pltpu.SemaphoreType.DMA((2,))],
        leave=pl.BlockSpec(memory_space=pltpu.HBM),
    )(jnp.asarray(plane_table()), back)
    return final.reshape(2, PLANES, CY, NZ)


def solution(mesh):
    in_specs = (
        P(("slab", "pencil")),
        P(("slab", "pencil")),
        P(("slab", "pencil")),
        P(None, ("slab", "pencil")),
        P(("slab", "pencil")),
        P(("slab", "pencil")),
        P(("slab", "pencil")),
        P(("slab", "pencil")),
    )
    out_specs = P(None, "slab", "pencil", None)
    return jax.shard_map(local, mesh=mesh, in_specs=in_specs, out_specs=out_specs, check_vma=False)
```

```python
import math

import jax
import jax.numpy as jnp
import numpy as np
from jax import lax
from jax.experimental import pallas as pl
from jax.experimental.pallas import tpu as pltpu
from jax.sharding import PartitionSpec as P

NX = 2048
GHOST = 3
CY = 8
NZ = 128
SLABS = 64
PLANES = 32
LANES = 128
ROWS = 32
PIECES = 11
EXT = 40
GROUPS = EXT // 8
WIDE = CY + 2 * GHOST
VMEM = 40 * 1024 * 1024


def split2(value):
    high = value.astype(jnp.bfloat16).astype(jnp.float32)
    return [high, value - high]


def bucket_kernel(live, *refs):
    sources, out, staged = refs[:7], refs[7], refs[8:15]
    shifts, pieces, chosen, counts, left, right, arrivals = refs[15:]
    copies = [
        pltpu.make_async_copy(source, place, arrivals.at[number])
        for number, (source, place) in enumerate(zip(sources, staged, strict=True))
    ]
    for copy in copies:
        copy.start()
    dest, offsets, cell_x, cell_y, cell_z, radius_bin, masses = staged
    copies[0].wait()
    slab = lax.broadcasted_iota(jnp.int32, (SLABS, LANES), 0)
    for k in range(ROWS):
        chosen[k * SLABS : (k + 1) * SLABS] = jnp.where(
            slab == dest[k : k + 1, :], 1.0, 0.0
        ).astype(jnp.bfloat16)
    first = lax.broadcasted_iota(jnp.int32, (LANES, 2 * LANES), 0)
    second = lax.broadcasted_iota(jnp.int32, (LANES, 2 * LANES), 1)
    before = jnp.where((first < second) | (second >= LANES), 1.0, 0.0).astype(jnp.bfloat16)
    counts[...] = jnp.dot(chosen[...], before, preferred_element_type=jnp.float32)
    for copy in copies[1:]:
        copy.wait()
    for axis in range(3):
        for k in range(ROWS):
            shifts[axis, k : k + 1, :] = offsets[
                axis : axis + 1, k * LANES : (k + 1) * LANES
            ]
    row = lax.broadcasted_iota(jnp.int32, (ROWS, LANES), 0)
    lane = lax.broadcasted_iota(jnp.int32, (ROWS, LANES), 1)
    weighted = jnp.where(row * LANES + lane < live[0], masses[...], 0.0)
    held = [
        (cell_x[...] + PLANES * radius_bin[...]).astype(jnp.float32),
        cell_y[...].astype(jnp.float32),
        cell_z[...].astype(jnp.float32),
        *split2(shifts[0]),
        *split2(shifts[1]),
        *split2(shifts[2]),
        *split2(weighted),
    ]
    for number, piece in enumerate(held):
        pieces[number] = piece
    base = jnp.zeros((SLABS, LANES), jnp.float32)
    pair = lax.broadcasted_iota(jnp.int32, (SLABS // 2, LANES), 0)
    low = lax.broadcasted_iota(jnp.int32, (2 * LANES, LANES), 0)
    for k in range(ROWS):
        target = dest[k : k + 1, :]
        found = counts[k * SLABS : (k + 1) * SLABS, :]
        rank = jnp.sum(
            jnp.where(slab == target, found[:, :LANES] + base, 0.0), axis=0, keepdims=True
        )
        base = base + found[:, LANES:]
        slot = jnp.right_shift(target, 5) * LANES + rank.astype(jnp.int32)
        span = slice(k * LANES, (k + 1) * LANES)
        right[:, span] = jnp.where(low == slot, 1.0, 0.0).astype(jnp.bfloat16)
        mask = pair == jnp.bitwise_and(target, SLABS // 2 - 1)
        for number in range(PIECES):
            left[number * ROWS : (number + 1) * ROWS, span] = jnp.where(
                mask, pieces[number, k : k + 1, :], 0.0
            ).astype(jnp.bfloat16)
    sent = lax.dot_general(
        left[...], right[...], (((1,), (1,)), ((), ())), preferred_element_type=jnp.float32
    )
    part = [sent[number * ROWS : (number + 1) * ROWS] for number in range(PIECES)]
    bins = jnp.floor(part[0] * (1.0 / PLANES))
    values = [
        (part[0] - PLANES * bins) + (part[3] + part[4]),
        part[1] + (part[5] + part[6]),
        part[2] + (part[7] + part[8]),
        part[9] + part[10],
        1.0 + 0.5 * bins,
    ]
    for field, value in enumerate(values):
        span = slice(field * LANES, (field + 1) * LANES)
        out[: SLABS // 2, 0, span] = value[:, :LANES]
        out[SLABS // 2 :, 0, span] = value[:, LANES:]


def tap_sum(position, inverse):
    fraction = position - jnp.floor(position)
    total = jnp.zeros_like(position)
    for tap in range(-GHOST, GHOST + 1):
        gap = (tap + 0.5 - fraction) * inverse
        bump = jnp.maximum(1.0 - gap * gap, 0.0)
        total = total + bump * bump
    return total


def bump_of(gap):
    value = jnp.maximum(1.0 - gap * gap, 0.0)
    return value * value


def around(gap):
    gap = jnp.abs(gap)
    return jnp.minimum(gap, NZ - gap)


BLOCK = 16


def deposit_rows(arrived, held, total, wanted):
    def field(number):
        return arrived[:, 0, number * LANES : (number + 1) * LANES]

    inverse = 1.0 / jnp.maximum(field(4), 1.0)
    held[0] = field(0)
    held[1] = field(1)
    held[2] = field(2)
    held[3] = inverse
    held[4] = field(3) / (tap_sum(held[0], inverse) * tap_sum(held[1], inverse))
    held[5] = 1.0 / tap_sum(held[2], inverse)
    total[...] = jnp.zeros_like(total)
    wide = BLOCK * LANES
    first = lax.broadcasted_iota(jnp.int32, (EXT, wide), 0).astype(jnp.float32) + (0.5 - GHOST)
    second = lax.broadcasted_iota(jnp.int32, (16, wide), 0).astype(jnp.float32) + (0.5 - GHOST)
    third = lax.broadcasted_iota(jnp.int32, (NZ, wide), 0).astype(jnp.float32) + 0.5

    def step(index, carry):
        def row(field):
            return jnp.concatenate(
                [held[field, pl.ds(index * BLOCK + part, 1), :] for part in range(BLOCK)], axis=1
            )

        scale = row(3)
        along_first = bump_of((first - row(0)) * scale) * row(4)
        along_second = bump_of((second - row(1)) * scale)
        away = third - row(2)
        away = jnp.concatenate([around(away[:8]), away[8 : NZ - 8], around(away[NZ - 8 :])], axis=0)
        depth = (bump_of(away * scale) * row(5)).astype(jnp.bfloat16)
        plane = jnp.concatenate(
            [along_first * along_second[y : y + 1, :] for y in wanted], axis=0
        ).astype(jnp.bfloat16)
        total[...] += lax.dot_general(
            plane, depth, (((1,), (1,)), ((), ())), preferred_element_type=jnp.float32
        )
        return carry

    lax.fori_loop(0, SLABS // BLOCK, step, 0, unroll=2)


def rim_kernel(arrived, lower, upper, held, total):
    deposit_rows(arrived, held, total, [*range(GHOST), *range(GHOST + CY, WIDE)])
    lower[...] = total[: GHOST * EXT]
    upper[...] = total[GHOST * EXT :]


def inner_kernel(arrived, tables, inner, table, held, arrival):
    copy = pltpu.make_async_copy(tables.at[lax.axis_index("slab") % 8], table, arrival)
    copy.start()
    deposit_rows(arrived, held, inner, range(GHOST, GHOST + CY))
    copy.wait()


def join_kernel(inner, before, after, out):
    for y in range(CY):
        for group in range(GROUPS):
            value = inner[y * EXT + group * 8 : y * EXT + group * 8 + 8]
            if y < GHOST:
                at = y * EXT + group * 8
                value = value + before[at : at + 8]
            if y >= CY - GHOST:
                at = (y - CY + GHOST) * EXT + group * 8
                value = value + after[at : at + 8]
            out[y * 8 : y * 8 + 8, 0, group * LANES : (group + 1) * LANES] = value


def slab_kernel(table, value, out):
    for group in range(GROUPS - 1):
        rows = value[:, 0, group * LANES : (group + 1) * LANES]
        if group == 0:
            last = value[:, 0, (GROUPS - 1) * LANES :]
            rows = rows + jnp.concatenate([last[SLABS - 1 :], last[: SLABS - 1]], axis=0)
        result = jnp.dot(
            table[group], rows, precision=lax.Precision.HIGHEST, preferred_element_type=jnp.float32
        )
        out[:, group, :] = result[:SLABS]
        out[:, GROUPS - 1 + group, :] = result[SLABS:]


def plane_kernel(table, value, out, held, leaves):
    rows = jnp.concatenate(
        [value[y * 8 : y * 8 + 8].reshape(SLABS, LANES) for y in range(CY)], axis=1
    )
    copies = []
    for part in range(2):
        span = pl.ds(part * PLANES, PLANES)
        result = jnp.dot(
            table[span, :], rows, precision=lax.Precision.HIGHEST, preferred_element_type=jnp.float32
        )
        for y in range(CY):
            held[span, y, :] = result[:, y * LANES : (y + 1) * LANES]
        copies.append(pltpu.make_async_copy(held.at[span], out.at[span], leaves.at[part]))
        copies[part].start()
    for copy in copies:
        copy.wait()


def slab_tables():
    device = np.arange(SLABS)
    frequency = np.zeros(SLABS, np.int64)
    for bit in range(6):
        frequency += (device >> bit & 1) << 5 - bit
    offset = np.arange(8)[:, None] + 8 * np.arange(4)[None, :] - GHOST
    cell = PLANES * device[None, None, None, :] + offset[:, :, None, None]
    angle = 2.0 * np.pi * (frequency[None, None, :, None] * cell % NX) / NX
    table = np.concatenate([np.cos(angle), -np.sin(angle)], axis=2)
    return (table / math.sqrt(NX)).astype(np.float32)


def plane_table():
    offset = np.arange(8)[:, None] + 8 * np.arange(4)[None, :] - GHOST
    angle = 2.0 * np.pi * (np.arange(PLANES)[:, None, None] * offset[None] % PLANES) / PLANES
    real = np.stack([np.cos(angle), np.sin(angle)], axis=2)
    imag = np.stack([-np.sin(angle), np.cos(angle)], axis=2)
    return np.stack([real, imag]).reshape(2 * PLANES, 8 * 2 * 4).astype(np.float32)


def call(kernel, out, scratch=(), specs=None, leave=None, flops=0, moved=0):
    return pl.pallas_call(
        kernel,
        out_shape=out,
        **({} if specs is None else {"in_specs": specs}),
        **({} if leave is None else {"out_specs": leave}),
        scratch_shapes=list(scratch),
        compiler_params=pltpu.CompilerParams(vmem_limit_bytes=VMEM),
        cost_estimate=pl.CostEstimate(flops=flops, bytes_accessed=moved, transcendentals=0),
    )


def shape(*dims):
    return jax.ShapeDtypeStruct(dims, jnp.float32)


def bucket(live_counts, cell_x, cell_y, cell_z, offsets, radius_bin, masses, slab_dest):
    block = (ROWS, LANES)
    sources = [slab_dest.reshape(block), offsets] + [
        value.reshape(block) for value in (cell_x, cell_y, cell_z, radius_bin, masses)
    ]
    return call(
        bucket_kernel,
        shape(SLABS, 1, 5 * LANES),
        [pltpu.VMEM(value.shape, value.dtype) for value in sources]
        + [
            pltpu.VMEM((3, ROWS, LANES), jnp.float32),
            pltpu.VMEM((PIECES, ROWS, LANES), jnp.float32),
            pltpu.VMEM((ROWS * SLABS, LANES), jnp.bfloat16),
            pltpu.VMEM((ROWS * SLABS, 2 * LANES), jnp.float32),
            pltpu.VMEM((PIECES * ROWS, ROWS * LANES), jnp.bfloat16),
            pltpu.VMEM((2 * LANES, ROWS * LANES), jnp.bfloat16),
            pltpu.SemaphoreType.DMA((7,)),
        ],
        [pl.BlockSpec(memory_space=pltpu.SMEM)] + [pl.BlockSpec(memory_space=pltpu.HBM)] * 7,
        flops=10**9,
        moved=10**6,
    )(live_counts, *[pltpu.with_memory_space_constraint(value, pltpu.HBM) for value in sources])


HELD = pltpu.VMEM((6, SLABS, LANES), jnp.float32)


def deposit_rims(arrived):
    rim = shape(GHOST * EXT, NZ)
    scratch = [HELD, pltpu.VMEM((2 * GHOST * EXT, NZ), jnp.float32)]
    return call(rim_kernel, (rim, rim), scratch, flops=5 * 10**8, moved=10**6)(arrived)


def deposit_inner(arrived):
    tables = pltpu.with_memory_space_constraint(jnp.asarray(slab_tables()), pltpu.HBM)
    return call(
        inner_kernel,
        (shape(CY * EXT, NZ), shape(*tables.shape[1:])),
        [HELD, pltpu.SemaphoreType.DMA],
        [pl.BlockSpec(memory_space=pltpu.VMEM), pl.BlockSpec(memory_space=pltpu.HBM)],
        flops=10**9,
        moved=10**6,
    )(arrived, tables)


def exchanged(value):
    return lax.all_to_all(value, "slab", split_axis=0, concat_axis=0, tiled=True)


def local(cell_x, cell_y, cell_z, offsets, radius_bin, masses, slab_dest, live_counts):
    outgoing = bucket(
        live_counts, cell_x, cell_y, cell_z, offsets, radius_bin, masses, slab_dest
    )
    arrived = exchanged(outgoing)
    lower, upper = deposit_rims(arrived)
    count = lax.axis_size("pencil")
    up = [(i, (i + 1) % count) for i in range(count)]
    before = lax.ppermute(upper, "pencil", up)
    after = lax.ppermute(lower, "pencil", [(j, i) for i, j in up])
    inner, table = deposit_inner(arrived)
    joined = call(join_kernel, shape(SLABS, 1, GROUPS * LANES))(inner, before, after)
    crossing = exchanged(joined)
    partial = call(slab_kernel, shape(SLABS, 2 * (GROUPS - 1), LANES))(table, crossing)
    back = exchanged(partial)
    final = call(
        plane_kernel,
        shape(2 * PLANES, CY, NZ),
        [pltpu.VMEM((2 * PLANES, CY, NZ), jnp.float32), pltpu.SemaphoreType.DMA((2,))],
        leave=pl.BlockSpec(memory_space=pltpu.HBM),
    )(jnp.asarray(plane_table()), back)
    return final.reshape(2, PLANES, CY, NZ)


def solution(mesh):
    in_specs = (
        P(("slab", "pencil")),
        P(("slab", "pencil")),
        P(("slab", "pencil")),
        P(None, ("slab", "pencil")),
        P(("slab", "pencil")),
        P(("slab", "pencil")),
        P(("slab", "pencil")),
        P(("slab", "pencil")),
    )
    out_specs = P(None, "slab", "pencil", None)
    return jax.shard_map(local, mesh=mesh, in_specs=in_specs, out_specs=out_specs, check_vma=False)
```

```python
import math

import jax
import jax.numpy as jnp
import numpy as np
from jax import lax
from jax.experimental import pallas as pl
from jax.experimental.pallas import tpu as pltpu
from jax.sharding import PartitionSpec as P

NX = 2048
GHOST = 3
CY = 8
NZ = 128
SLABS = 64
PLANES = 32
LANES = 128
ROWS = 32
PIECES = 11
EXT = 40
GROUPS = EXT // 8
WIDE = CY + 2 * GHOST
VMEM = 40 * 1024 * 1024


def split2(value):
    high = value.astype(jnp.bfloat16).astype(jnp.float32)
    return [high, value - high]


def bucket_kernel(live, *refs):
    sources, out, staged = refs[:7], refs[7], refs[8:15]
    shifts, pieces, chosen, counts, arrivals = refs[15:]
    copies = [
        pltpu.make_async_copy(source, place, arrivals.at[number])
        for number, (source, place) in enumerate(zip(sources, staged, strict=True))
    ]
    for copy in copies:
        copy.start()
    dest, offsets, cell_x, cell_y, cell_z, radius_bin, masses = staged
    copies[0].wait()
    slab = lax.broadcasted_iota(jnp.int32, (SLABS, LANES), 0)
    for k in range(ROWS):
        chosen[k * SLABS : (k + 1) * SLABS] = jnp.where(
            slab == dest[k : k + 1, :], 1.0, 0.0
        ).astype(jnp.bfloat16)
    first = lax.broadcasted_iota(jnp.int32, (LANES, 2 * LANES), 0)
    second = lax.broadcasted_iota(jnp.int32, (LANES, 2 * LANES), 1)
    before = jnp.where((first < second) | (second >= LANES), 1.0, 0.0).astype(jnp.bfloat16)
    counts[...] = jnp.dot(chosen[...], before, preferred_element_type=jnp.float32)
    for copy in copies[1:]:
        copy.wait()
    for axis in range(3):
        for k in range(ROWS):
            shifts[axis, k : k + 1, :] = offsets[
                axis : axis + 1, k * LANES : (k + 1) * LANES
            ]
    row = lax.broadcasted_iota(jnp.int32, (ROWS, LANES), 0)
    lane = lax.broadcasted_iota(jnp.int32, (ROWS, LANES), 1)
    weighted = jnp.where(row * LANES + lane < live[0], masses[...], 0.0)
    held = [
        (cell_x[...] + PLANES * radius_bin[...]).astype(jnp.float32),
        cell_y[...].astype(jnp.float32),
        cell_z[...].astype(jnp.float32),
        *split2(shifts[0]),
        *split2(shifts[1]),
        *split2(shifts[2]),
        *split2(weighted),
    ]
    for number, piece in enumerate(held):
        pieces[number] = piece
    base = jnp.zeros((SLABS, LANES), jnp.float32)
    low = lax.broadcasted_iota(jnp.int32, (LANES, LANES), 0)
    lefts, rights, sent = [], [], 0.0
    for k in range(ROWS):
        target = dest[k : k + 1, :]
        found = counts[k * SLABS : (k + 1) * SLABS, :]
        mask = slab == target
        rank = jnp.sum(jnp.where(mask, found[:, :LANES] + base, 0.0), axis=0, keepdims=True)
        base = base + found[:, LANES:]
        rights.append(jnp.where(low == rank.astype(jnp.int32), 1.0, 0.0).astype(jnp.bfloat16))
        lefts.append(
            jnp.concatenate(
                [jnp.where(mask, pieces[number, k : k + 1, :], 0.0) for number in range(PIECES)], axis=0
            ).astype(jnp.bfloat16)
        )
        if len(lefts) == 8:
            sent = sent + lax.dot_general(
                jnp.concatenate(lefts, axis=1),
                jnp.concatenate(rights, axis=1),
                (((1,), (1,)), ((), ())),
                preferred_element_type=jnp.float32,
            )
            lefts, rights = [], []
    part = [sent[number * SLABS : (number + 1) * SLABS] for number in range(PIECES)]
    bins = jnp.floor(part[0] * (1.0 / PLANES))
    values = [
        (part[0] - PLANES * bins) + (part[3] + part[4]),
        part[1] + (part[5] + part[6]),
        part[2] + (part[7] + part[8]),
        part[9] + part[10],
        1.0 + 0.5 * bins,
    ]
    for field, value in enumerate(values):
        out[:, 0, field * LANES : (field + 1) * LANES] = value


def tap_sum(position, inverse):
    fraction = position - jnp.floor(position)
    total = jnp.zeros_like(position)
    for tap in range(-GHOST, GHOST + 1):
        gap = (tap + 0.5 - fraction) * inverse
        bump = jnp.maximum(1.0 - gap * gap, 0.0)
        total = total + bump * bump
    return total


def bump_of(gap):
    value = jnp.maximum(1.0 - gap * gap, 0.0)
    return value * value


def around(gap):
    gap = jnp.abs(gap)
    return jnp.minimum(gap, NZ - gap)


BLOCK = 16


def deposit_rows(arrived, held, total, wanted):
    def field(number):
        return arrived[:, 0, number * LANES : (number + 1) * LANES]

    inverse = 1.0 / jnp.maximum(field(4), 1.0)
    held[0] = field(0)
    held[1] = field(1)
    held[2] = field(2)
    held[3] = inverse
    held[4] = field(3) / (tap_sum(held[0], inverse) * tap_sum(held[1], inverse))
    held[5] = 1.0 / tap_sum(held[2], inverse)
    total[...] = jnp.zeros_like(total)
    wide = BLOCK * LANES
    first = lax.broadcasted_iota(jnp.int32, (EXT, wide), 0).astype(jnp.float32) + (0.5 - GHOST)
    second = lax.broadcasted_iota(jnp.int32, (16, wide), 0).astype(jnp.float32) + (0.5 - GHOST)
    third = lax.broadcasted_iota(jnp.int32, (NZ, wide), 0).astype(jnp.float32) + 0.5

    def step(index, carry):
        def row(field):
            return jnp.concatenate(
                [held[field, pl.ds(index * BLOCK + part, 1), :] for part in range(BLOCK)], axis=1
            )

        scale = row(3)
        along_first = bump_of((first - row(0)) * scale) * row(4)
        along_second = bump_of((second - row(1)) * scale)
        away = third - row(2)
        away = jnp.concatenate([around(away[:8]), away[8 : NZ - 8], around(away[NZ - 8 :])], axis=0)
        depth = (bump_of(away * scale) * row(5)).astype(jnp.bfloat16)
        plane = jnp.concatenate(
            [along_first * along_second[y : y + 1, :] for y in wanted], axis=0
        ).astype(jnp.bfloat16)
        total[...] += lax.dot_general(
            plane, depth, (((1,), (1,)), ((), ())), preferred_element_type=jnp.float32
        )
        return carry

    lax.fori_loop(0, SLABS // BLOCK, step, 0, unroll=2)


def rim_kernel(arrived, lower, upper, held, total):
    deposit_rows(arrived, held, total, [*range(GHOST), *range(GHOST + CY, WIDE)])
    lower[...] = total[: GHOST * EXT]
    upper[...] = total[GHOST * EXT :]


def inner_kernel(arrived, tables, inner, table, held, arrival):
    copy = pltpu.make_async_copy(tables.at[lax.axis_index("slab") % 8], table, arrival)
    copy.start()
    deposit_rows(arrived, held, inner, range(GHOST, GHOST + CY))
    copy.wait()


def join_kernel(inner, before, after, out):
    for y in range(CY):
        for group in range(GROUPS):
            value = inner[y * EXT + group * 8 : y * EXT + group * 8 + 8]
            if y < GHOST:
                at = y * EXT + group * 8
                value = value + before[at : at + 8]
            if y >= CY - GHOST:
                at = (y - CY + GHOST) * EXT + group * 8
                value = value + after[at : at + 8]
            out[y * 8 : y * 8 + 8, 0, group * LANES : (group + 1) * LANES] = value


def slab_kernel(table, value, out):
    for group in range(GROUPS - 1):
        rows = value[:, 0, group * LANES : (group + 1) * LANES]
        if group == 0:
            last = value[:, 0, (GROUPS - 1) * LANES :]
            rows = rows + jnp.concatenate([last[SLABS - 1 :], last[: SLABS - 1]], axis=0)
        result = jnp.dot(
            table[group], rows, precision=lax.Precision.HIGHEST, preferred_element_type=jnp.float32
        )
        out[:, group, :] = result[:SLABS]
        out[:, GROUPS - 1 + group, :] = result[SLABS:]


def plane_kernel(table, value, out, held, leaves):
    rows = jnp.concatenate(
        [value[y * 8 : y * 8 + 8].reshape(SLABS, LANES) for y in range(CY)], axis=1
    )
    copies = []
    for part in range(2):
        span = pl.ds(part * PLANES, PLANES)
        result = jnp.dot(
            table[span, :], rows, precision=lax.Precision.HIGHEST, preferred_element_type=jnp.float32
        )
        for y in range(CY):
            held[span, y, :] = result[:, y * LANES : (y + 1) * LANES]
        copies.append(pltpu.make_async_copy(held.at[span], out.at[span], leaves.at[part]))
        copies[part].start()
    for copy in copies:
        copy.wait()


def slab_tables():
    device = np.arange(SLABS)
    frequency = np.zeros(SLABS, np.int64)
    for bit in range(6):
        frequency += (device >> bit & 1) << 5 - bit
    offset = np.arange(8)[:, None] + 8 * np.arange(4)[None, :] - GHOST
    cell = PLANES * device[None, None, None, :] + offset[:, :, None, None]
    angle = 2.0 * np.pi * (frequency[None, None, :, None] * cell % NX) / NX
    table = np.concatenate([np.cos(angle), -np.sin(angle)], axis=2)
    return (table / math.sqrt(NX)).astype(np.float32)


def plane_table():
    offset = np.arange(8)[:, None] + 8 * np.arange(4)[None, :] - GHOST
    angle = 2.0 * np.pi * (np.arange(PLANES)[:, None, None] * offset[None] % PLANES) / PLANES
    real = np.stack([np.cos(angle), np.sin(angle)], axis=2)
    imag = np.stack([-np.sin(angle), np.cos(angle)], axis=2)
    return np.stack([real, imag]).reshape(2 * PLANES, 8 * 2 * 4).astype(np.float32)


def call(kernel, out, scratch=(), specs=None, leave=None, flops=0, moved=0):
    return pl.pallas_call(
        kernel,
        out_shape=out,
        **({} if specs is None else {"in_specs": specs}),
        **({} if leave is None else {"out_specs": leave}),
        scratch_shapes=list(scratch),
        compiler_params=pltpu.CompilerParams(vmem_limit_bytes=VMEM),
        cost_estimate=pl.CostEstimate(flops=flops, bytes_accessed=moved, transcendentals=0),
    )


def shape(*dims):
    return jax.ShapeDtypeStruct(dims, jnp.float32)


def bucket(live_counts, cell_x, cell_y, cell_z, offsets, radius_bin, masses, slab_dest):
    block = (ROWS, LANES)
    sources = [slab_dest.reshape(block), offsets] + [
        value.reshape(block) for value in (cell_x, cell_y, cell_z, radius_bin, masses)
    ]
    return call(
        bucket_kernel,
        shape(SLABS, 1, 5 * LANES),
        [pltpu.VMEM(value.shape, value.dtype) for value in sources]
        + [
            pltpu.VMEM((3, ROWS, LANES), jnp.float32),
            pltpu.VMEM((PIECES, ROWS, LANES), jnp.float32),
            pltpu.VMEM((ROWS * SLABS, LANES), jnp.bfloat16),
            pltpu.VMEM((ROWS * SLABS, 2 * LANES), jnp.float32),
            pltpu.SemaphoreType.DMA((7,)),
        ],
        [pl.BlockSpec(memory_space=pltpu.SMEM)] + [pl.BlockSpec(memory_space=pltpu.HBM)] * 7,
        flops=10**9,
        moved=10**6,
    )(live_counts, *[pltpu.with_memory_space_constraint(value, pltpu.HBM) for value in sources])


HELD = pltpu.VMEM((6, SLABS, LANES), jnp.float32)


def deposit_rims(arrived):
    rim = shape(GHOST * EXT, NZ)
    scratch = [HELD, pltpu.VMEM((2 * GHOST * EXT, NZ), jnp.float32)]
    return call(rim_kernel, (rim, rim), scratch, flops=5 * 10**8, moved=10**6)(arrived)


def deposit_inner(arrived):
    tables = pltpu.with_memory_space_constraint(jnp.asarray(slab_tables()), pltpu.HBM)
    return call(
        inner_kernel,
        (shape(CY * EXT, NZ), shape(*tables.shape[1:])),
        [HELD, pltpu.SemaphoreType.DMA],
        [pl.BlockSpec(memory_space=pltpu.VMEM), pl.BlockSpec(memory_space=pltpu.HBM)],
        flops=10**9,
        moved=10**6,
    )(arrived, tables)


def exchanged(value):
    return lax.all_to_all(value, "slab", split_axis=0, concat_axis=0, tiled=True)


def local(cell_x, cell_y, cell_z, offsets, radius_bin, masses, slab_dest, live_counts):
    outgoing = bucket(
        live_counts, cell_x, cell_y, cell_z, offsets, radius_bin, masses, slab_dest
    )
    arrived = exchanged(outgoing)
    lower, upper = deposit_rims(arrived)
    count = lax.axis_size("pencil")
    up = [(i, (i + 1) % count) for i in range(count)]
    before = lax.ppermute(upper, "pencil", up)
    after = lax.ppermute(lower, "pencil", [(j, i) for i, j in up])
    inner, table = deposit_inner(arrived)
    joined = call(join_kernel, shape(SLABS, 1, GROUPS * LANES))(inner, before, after)
    crossing = exchanged(joined)
    partial = call(slab_kernel, shape(SLABS, 2 * (GROUPS - 1), LANES))(table, crossing)
    back = exchanged(partial)
    final = call(
        plane_kernel,
        shape(2 * PLANES, CY, NZ),
        [pltpu.VMEM((2 * PLANES, CY, NZ), jnp.float32), pltpu.SemaphoreType.DMA((2,))],
        leave=pl.BlockSpec(memory_space=pltpu.HBM),
    )(jnp.asarray(plane_table()), back)
    return final.reshape(2, PLANES, CY, NZ)


def solution(mesh):
    in_specs = (
        P(("slab", "pencil")),
        P(("slab", "pencil")),
        P(("slab", "pencil")),
        P(None, ("slab", "pencil")),
        P(("slab", "pencil")),
        P(("slab", "pencil")),
        P(("slab", "pencil")),
        P(("slab", "pencil")),
    )
    out_specs = P(None, "slab", "pencil", None)
    return jax.shard_map(local, mesh=mesh, in_specs=in_specs, out_specs=out_specs, check_vma=False)
```

```python
import math

import jax
import jax.numpy as jnp
import numpy as np
from jax import lax
from jax.experimental import pallas as pl
from jax.experimental.pallas import tpu as pltpu
from jax.sharding import PartitionSpec as P

NX = 2048
GHOST = 3
CY = 8
NZ = 128
SLABS = 64
PLANES = 32
LANES = 128
ROWS = 32
PIECES = 11
EXT = 40
GROUPS = EXT // 8
WIDE = CY + 2 * GHOST
VMEM = 40 * 1024 * 1024


def split2(value):
    high = value.astype(jnp.bfloat16).astype(jnp.float32)
    return [high, value - high]


def bucket_kernel(live, *refs):
    sources, out, staged = refs[:7], refs[7], refs[8:15]
    shifts, pieces, chosen, counts, arrivals = refs[15:]
    copies = [
        pltpu.make_async_copy(source, place, arrivals.at[number])
        for number, (source, place) in enumerate(zip(sources, staged, strict=True))
    ]
    for copy in copies:
        copy.start()
    dest, offsets, cell_x, cell_y, cell_z, radius_bin, masses = staged
    copies[0].wait()
    slab = lax.broadcasted_iota(jnp.int32, (SLABS, LANES), 0)
    for k in range(ROWS):
        chosen[k * SLABS : (k + 1) * SLABS] = jnp.where(
            slab == dest[k : k + 1, :], 1.0, 0.0
        ).astype(jnp.bfloat16)
    first = lax.broadcasted_iota(jnp.int32, (LANES, 2 * LANES), 0)
    second = lax.broadcasted_iota(jnp.int32, (LANES, 2 * LANES), 1)
    before = jnp.where((first < second) | (second >= LANES), 1.0, 0.0).astype(jnp.bfloat16)
    counts[...] = jnp.dot(chosen[...], before, preferred_element_type=jnp.float32)
    for copy in copies[1:]:
        copy.wait()
    for axis in range(3):
        for k in range(ROWS):
            shifts[axis, k : k + 1, :] = offsets[
                axis : axis + 1, k * LANES : (k + 1) * LANES
            ]
    row = lax.broadcasted_iota(jnp.int32, (ROWS, LANES), 0)
    lane = lax.broadcasted_iota(jnp.int32, (ROWS, LANES), 1)
    weighted = jnp.where(row * LANES + lane < live[0], masses[...], 0.0)
    held = [
        (cell_x[...] + PLANES * radius_bin[...]).astype(jnp.float32),
        cell_y[...].astype(jnp.float32),
        cell_z[...].astype(jnp.float32),
        *split2(shifts[0]),
        *split2(shifts[1]),
        *split2(shifts[2]),
        *split2(weighted),
    ]
    for number, piece in enumerate(held):
        pieces[number] = piece
    base = jnp.zeros((SLABS, LANES), jnp.float32)
    low = lax.broadcasted_iota(jnp.int32, (LANES, LANES), 0)
    lefts, rights, sent = [], [], 0.0
    for k in range(ROWS):
        target = dest[k : k + 1, :]
        found = counts[k * SLABS : (k + 1) * SLABS, :]
        mask = slab == target
        rank = jnp.sum(jnp.where(mask, found[:, :LANES] + base, 0.0), axis=0, keepdims=True)
        base = base + found[:, LANES:]
        rights.append(jnp.where(low == rank.astype(jnp.int32), 1.0, 0.0).astype(jnp.bfloat16))
        lefts.append(
            jnp.concatenate(
                [jnp.where(mask, pieces[number, k : k + 1, :], 0.0) for number in range(PIECES)], axis=0
            ).astype(jnp.bfloat16)
        )
        if len(lefts) == 8:
            sent = sent + lax.dot_general(
                jnp.concatenate(lefts, axis=1),
                jnp.concatenate(rights, axis=1),
                (((1,), (1,)), ((), ())),
                preferred_element_type=jnp.float32,
            )
            lefts, rights = [], []
    part = [sent[number * SLABS : (number + 1) * SLABS] for number in range(PIECES)]
    bins = jnp.floor(part[0] * (1.0 / PLANES))
    values = [
        (part[0] - PLANES * bins) + (part[3] + part[4]),
        part[1] + (part[5] + part[6]),
        part[2] + (part[7] + part[8]),
        part[9] + part[10],
        1.0 + 0.5 * bins,
    ]
    for field, value in enumerate(values):
        out[:, 0, field * LANES : (field + 1) * LANES] = value


def tap_sum(position, inverse):
    fraction = position - jnp.floor(position)
    total = jnp.zeros_like(position)
    for tap in range(-GHOST, GHOST + 1):
        gap = (tap + 0.5 - fraction) * inverse
        bump = jnp.maximum(1.0 - gap * gap, 0.0)
        total = total + bump * bump
    return total


def bump_of(gap):
    value = jnp.maximum(1.0 - gap * gap, 0.0)
    return value * value


def around(gap):
    gap = jnp.abs(gap)
    return jnp.minimum(gap, NZ - gap)


BLOCK = 16


def add_rows(held, depth, fill, total, wanted):
    total[...] = jnp.zeros_like(total)
    wide = BLOCK * LANES
    first = lax.broadcasted_iota(jnp.int32, (EXT, wide), 0).astype(jnp.float32) + (0.5 - GHOST)
    second = lax.broadcasted_iota(jnp.int32, (16, wide), 0).astype(jnp.float32) + (0.5 - GHOST)
    third = lax.broadcasted_iota(jnp.int32, (NZ, wide), 0).astype(jnp.float32) + 0.5

    def step(index, carry):
        def row(field):
            return jnp.concatenate(
                [held[field, pl.ds(index * BLOCK + part, 1), :] for part in range(BLOCK)], axis=1
            )

        span = pl.ds(pl.multiple_of(index * wide, wide), wide)
        scale = row(3)
        along_first = bump_of((first - row(0)) * scale) * row(4)
        along_second = bump_of((second - row(1)) * scale)
        if fill:
            away = third - row(2)
            away = jnp.concatenate(
                [around(away[:8]), away[8 : NZ - 8], around(away[NZ - 8 :])], axis=0
            )
            along_third = (bump_of(away * scale) * row(5)).astype(jnp.bfloat16)
            depth[:, span] = along_third
        else:
            along_third = depth[:, span]
        plane = jnp.concatenate(
            [along_first * along_second[y : y + 1, :] for y in wanted], axis=0
        ).astype(jnp.bfloat16)
        total[...] += lax.dot_general(
            plane, along_third, (((1,), (1,)), ((), ())), preferred_element_type=jnp.float32
        )
        return carry

    lax.fori_loop(0, SLABS // BLOCK, step, 0, unroll=2)


def rim_kernel(arrived, lower, upper, held, depth, total):
    def field(number):
        return arrived[:, 0, number * LANES : (number + 1) * LANES]

    inverse = 1.0 / jnp.maximum(field(4), 1.0)
    held[0] = field(0)
    held[1] = field(1)
    held[2] = field(2)
    held[3] = inverse
    held[4] = field(3) / (tap_sum(held[0], inverse) * tap_sum(held[1], inverse))
    held[5] = 1.0 / tap_sum(held[2], inverse)
    add_rows(held, depth, True, total, [*range(GHOST), *range(GHOST + CY, WIDE)])
    lower[...] = total[: GHOST * EXT]
    upper[...] = total[GHOST * EXT :]


def inner_kernel(held, depth, tables, inner, table, arrival):
    copy = pltpu.make_async_copy(tables.at[lax.axis_index("slab") % 8], table, arrival)
    copy.start()
    add_rows(held, depth, False, inner, range(GHOST, GHOST + CY))
    copy.wait()


def join_kernel(inner, before, after, out):
    for y in range(CY):
        for group in range(GROUPS):
            value = inner[y * EXT + group * 8 : y * EXT + group * 8 + 8]
            if y < GHOST:
                at = y * EXT + group * 8
                value = value + before[at : at + 8]
            if y >= CY - GHOST:
                at = (y - CY + GHOST) * EXT + group * 8
                value = value + after[at : at + 8]
            out[y * 8 : y * 8 + 8, 0, group * LANES : (group + 1) * LANES] = value


def slab_kernel(table, value, out):
    for group in range(GROUPS - 1):
        rows = value[:, 0, group * LANES : (group + 1) * LANES]
        if group == 0:
            last = value[:, 0, (GROUPS - 1) * LANES :]
            rows = rows + jnp.concatenate([last[SLABS - 1 :], last[: SLABS - 1]], axis=0)
        result = jnp.dot(
            table[group], rows, precision=lax.Precision.HIGHEST, preferred_element_type=jnp.float32
        )
        out[:, group, :] = result[:SLABS]
        out[:, GROUPS - 1 + group, :] = result[SLABS:]


def plane_kernel(table, value, out, held, leaves):
    rows = jnp.concatenate(
        [value[y * 8 : y * 8 + 8].reshape(SLABS, LANES) for y in range(CY)], axis=1
    )
    copies = []
    for part in range(2):
        span = pl.ds(part * PLANES, PLANES)
        result = jnp.dot(
            table[span, :], rows, precision=lax.Precision.HIGHEST, preferred_element_type=jnp.float32
        )
        for y in range(CY):
            held[span, y, :] = result[:, y * LANES : (y + 1) * LANES]
        copies.append(pltpu.make_async_copy(held.at[span], out.at[span], leaves.at[part]))
        copies[part].start()
    for copy in copies:
        copy.wait()


def slab_tables():
    device = np.arange(SLABS)
    frequency = np.zeros(SLABS, np.int64)
    for bit in range(6):
        frequency += (device >> bit & 1) << 5 - bit
    offset = np.arange(8)[:, None] + 8 * np.arange(4)[None, :] - GHOST
    cell = PLANES * device[None, None, None, :] + offset[:, :, None, None]
    angle = 2.0 * np.pi * (frequency[None, None, :, None] * cell % NX) / NX
    table = np.concatenate([np.cos(angle), -np.sin(angle)], axis=2)
    return (table / math.sqrt(NX)).astype(np.float32)


def plane_table():
    offset = np.arange(8)[:, None] + 8 * np.arange(4)[None, :] - GHOST
    angle = 2.0 * np.pi * (np.arange(PLANES)[:, None, None] * offset[None] % PLANES) / PLANES
    real = np.stack([np.cos(angle), np.sin(angle)], axis=2)
    imag = np.stack([-np.sin(angle), np.cos(angle)], axis=2)
    return np.stack([real, imag]).reshape(2 * PLANES, 8 * 2 * 4).astype(np.float32)


def call(kernel, out, scratch=(), specs=None, leave=None, flops=0, moved=0):
    return pl.pallas_call(
        kernel,
        out_shape=out,
        **({} if specs is None else {"in_specs": specs}),
        **({} if leave is None else {"out_specs": leave}),
        scratch_shapes=list(scratch),
        compiler_params=pltpu.CompilerParams(vmem_limit_bytes=VMEM),
        cost_estimate=pl.CostEstimate(flops=flops, bytes_accessed=moved, transcendentals=0),
    )


def shape(*dims):
    return jax.ShapeDtypeStruct(dims, jnp.float32)


def bucket(live_counts, cell_x, cell_y, cell_z, offsets, radius_bin, masses, slab_dest):
    block = (ROWS, LANES)
    sources = [slab_dest.reshape(block), offsets] + [
        value.reshape(block) for value in (cell_x, cell_y, cell_z, radius_bin, masses)
    ]
    return call(
        bucket_kernel,
        shape(SLABS, 1, 5 * LANES),
        [pltpu.VMEM(value.shape, value.dtype) for value in sources]
        + [
            pltpu.VMEM((3, ROWS, LANES), jnp.float32),
            pltpu.VMEM((PIECES, ROWS, LANES), jnp.float32),
            pltpu.VMEM((ROWS * SLABS, LANES), jnp.bfloat16),
            pltpu.VMEM((ROWS * SLABS, 2 * LANES), jnp.float32),
            pltpu.SemaphoreType.DMA((7,)),
        ],
        [pl.BlockSpec(memory_space=pltpu.SMEM)] + [pl.BlockSpec(memory_space=pltpu.HBM)] * 7,
        flops=10**9,
        moved=10**6,
    )(live_counts, *[pltpu.with_memory_space_constraint(value, pltpu.HBM) for value in sources])


def deposit_rims(arrived):
    rim = shape(GHOST * EXT, NZ)
    depth = jax.ShapeDtypeStruct((NZ, SLABS * LANES), jnp.bfloat16)
    return call(
        rim_kernel,
        (rim, rim, shape(6, SLABS, LANES), depth),
        [pltpu.VMEM((2 * GHOST * EXT, NZ), jnp.float32)],
        flops=5 * 10**8,
        moved=10**6,
    )(arrived)


def deposit_inner(held, depth):
    tables = pltpu.with_memory_space_constraint(jnp.asarray(slab_tables()), pltpu.HBM)
    here = pl.BlockSpec(memory_space=pltpu.VMEM)
    return call(
        inner_kernel,
        (shape(CY * EXT, NZ), shape(*tables.shape[1:])),
        [pltpu.SemaphoreType.DMA],
        [here, here, pl.BlockSpec(memory_space=pltpu.HBM)],
        flops=10**9,
        moved=10**6,
    )(held, depth, tables)


def exchanged(value):
    return lax.all_to_all(value, "slab", split_axis=0, concat_axis=0, tiled=True)


def local(cell_x, cell_y, cell_z, offsets, radius_bin, masses, slab_dest, live_counts):
    outgoing = bucket(
        live_counts, cell_x, cell_y, cell_z, offsets, radius_bin, masses, slab_dest
    )
    arrived = exchanged(outgoing)
    lower, upper, held, depth = deposit_rims(arrived)
    count = lax.axis_size("pencil")
    up = [(i, (i + 1) % count) for i in range(count)]
    before = lax.ppermute(upper, "pencil", up)
    after = lax.ppermute(lower, "pencil", [(j, i) for i, j in up])
    inner, table = deposit_inner(held, depth)
    joined = call(join_kernel, shape(SLABS, 1, GROUPS * LANES))(inner, before, after)
    crossing = exchanged(joined)
    partial = call(slab_kernel, shape(SLABS, 2 * (GROUPS - 1), LANES))(table, crossing)
    back = exchanged(partial)
    final = call(
        plane_kernel,
        shape(2 * PLANES, CY, NZ),
        [pltpu.VMEM((2 * PLANES, CY, NZ), jnp.float32), pltpu.SemaphoreType.DMA((2,))],
        leave=pl.BlockSpec(memory_space=pltpu.HBM),
    )(jnp.asarray(plane_table()), back)
    return final.reshape(2, PLANES, CY, NZ)


def solution(mesh):
    in_specs = (
        P(("slab", "pencil")),
        P(("slab", "pencil")),
        P(("slab", "pencil")),
        P(None, ("slab", "pencil")),
        P(("slab", "pencil")),
        P(("slab", "pencil")),
        P(("slab", "pencil")),
        P(("slab", "pencil")),
    )
    out_specs = P(None, "slab", "pencil", None)
    return jax.shard_map(local, mesh=mesh, in_specs=in_specs, out_specs=out_specs, check_vma=False)
```

```python
import math

import jax
import jax.numpy as jnp
import numpy as np
from jax import lax
from jax.experimental import pallas as pl
from jax.experimental.pallas import tpu as pltpu
from jax.sharding import PartitionSpec as P

NX = 2048
GHOST = 3
CY = 8
NZ = 128
SLABS = 64
PLANES = 32
LANES = 128
ROWS = 32
PIECES = 11
EXT = 40
GROUPS = EXT // 8
WIDE = CY + 2 * GHOST
VMEM = 40 * 1024 * 1024


def split2(value):
    high = value.astype(jnp.bfloat16).astype(jnp.float32)
    return [high, value - high]


def bucket_kernel(live, *refs):
    sources, out, staged = refs[:7], refs[7], refs[8:15]
    shifts, pieces, chosen, counts, arrivals = refs[15:]
    copies = [
        pltpu.make_async_copy(source, place, arrivals.at[number])
        for number, (source, place) in enumerate(zip(sources, staged, strict=True))
    ]
    for copy in copies:
        copy.start()
    dest, offsets, cell_x, cell_y, cell_z, radius_bin, masses = staged
    copies[0].wait()
    slab = lax.broadcasted_iota(jnp.int32, (SLABS, LANES), 0)
    for k in range(ROWS):
        chosen[k * SLABS : (k + 1) * SLABS] = jnp.where(
            slab == dest[k : k + 1, :], 1.0, 0.0
        ).astype(jnp.bfloat16)
    first = lax.broadcasted_iota(jnp.int32, (LANES, 2 * LANES), 0)
    second = lax.broadcasted_iota(jnp.int32, (LANES, 2 * LANES), 1)
    before = jnp.where((first < second) | (second >= LANES), 1.0, 0.0).astype(jnp.bfloat16)
    counts[...] = jnp.dot(chosen[...], before, preferred_element_type=jnp.float32)
    for copy in copies[1:]:
        copy.wait()
    for axis in range(3):
        for k in range(ROWS):
            shifts[axis, k : k + 1, :] = offsets[
                axis : axis + 1, k * LANES : (k + 1) * LANES
            ]
    row = lax.broadcasted_iota(jnp.int32, (ROWS, LANES), 0)
    lane = lax.broadcasted_iota(jnp.int32, (ROWS, LANES), 1)
    weighted = jnp.where(row * LANES + lane < live[0], masses[...], 0.0)
    held = [
        (cell_x[...] + PLANES * radius_bin[...]).astype(jnp.float32),
        cell_y[...].astype(jnp.float32),
        cell_z[...].astype(jnp.float32),
        *split2(shifts[0]),
        *split2(shifts[1]),
        *split2(shifts[2]),
        *split2(weighted),
    ]
    for number, piece in enumerate(held):
        pieces[number] = piece
    base = jnp.zeros((SLABS, LANES), jnp.float32)
    low = lax.broadcasted_iota(jnp.int32, (LANES, LANES), 0)
    lefts, rights, sent = [], [], 0.0
    for k in range(ROWS):
        target = dest[k : k + 1, :]
        found = counts[k * SLABS : (k + 1) * SLABS, :]
        mask = slab == target
        rank = jnp.sum(jnp.where(mask, found[:, :LANES] + base, 0.0), axis=0, keepdims=True)
        base = base + found[:, LANES:]
        rights.append(jnp.where(low == rank.astype(jnp.int32), 1.0, 0.0).astype(jnp.bfloat16))
        lefts.append(
            jnp.concatenate(
                [jnp.where(mask, pieces[number, k : k + 1, :], 0.0) for number in range(PIECES)], axis=0
            ).astype(jnp.bfloat16)
        )
        if len(lefts) == 4:
            sent = sent + lax.dot_general(
                jnp.concatenate(lefts, axis=1),
                jnp.concatenate(rights, axis=1),
                (((1,), (1,)), ((), ())),
                preferred_element_type=jnp.float32,
            )
            lefts, rights = [], []
    part = [sent[number * SLABS : (number + 1) * SLABS] for number in range(PIECES)]
    bins = jnp.floor(part[0] * (1.0 / PLANES))
    values = [
        (part[0] - PLANES * bins) + (part[3] + part[4]),
        part[1] + (part[5] + part[6]),
        part[2] + (part[7] + part[8]),
        part[9] + part[10],
        1.0 + 0.5 * bins,
    ]
    for field, value in enumerate(values):
        out[:, 0, field * LANES : (field + 1) * LANES] = value


def tap_sum(position, inverse):
    fraction = position - jnp.floor(position)
    total = jnp.zeros_like(position)
    for tap in range(-GHOST, GHOST + 1):
        gap = (tap + 0.5 - fraction) * inverse
        bump = jnp.maximum(1.0 - gap * gap, 0.0)
        total = total + bump * bump
    return total


def bump_of(gap):
    value = jnp.maximum(1.0 - gap * gap, 0.0)
    return value * value


def around(gap):
    gap = jnp.abs(gap)
    return jnp.minimum(gap, NZ - gap)


BLOCK = 16


def deposit_rows(arrived, held, total, wanted):
    def field(number):
        return arrived[:, 0, number * LANES : (number + 1) * LANES]

    inverse = 1.0 / jnp.maximum(field(4), 1.0)
    held[0] = field(0)
    held[1] = field(1)
    held[2] = field(2)
    held[3] = inverse
    held[4] = field(3) / (tap_sum(held[0], inverse) * tap_sum(held[1], inverse))
    held[5] = 1.0 / tap_sum(held[2], inverse)
    total[...] = jnp.zeros_like(total)
    wide = BLOCK * LANES
    first = lax.broadcasted_iota(jnp.int32, (EXT, wide), 0).astype(jnp.float32) + (0.5 - GHOST)
    second = lax.broadcasted_iota(jnp.int32, (16, wide), 0).astype(jnp.float32) + (0.5 - GHOST)
    third = lax.broadcasted_iota(jnp.int32, (NZ, wide), 0).astype(jnp.float32) + 0.5

    def step(index, carry):
        def row(field):
            return jnp.concatenate(
                [held[field, pl.ds(index * BLOCK + part, 1), :] for part in range(BLOCK)], axis=1
            )

        scale = row(3)
        along_first = bump_of((first - row(0)) * scale) * row(4)
        along_second = bump_of((second - row(1)) * scale)
        away = third - row(2)
        away = jnp.concatenate([around(away[:8]), away[8 : NZ - 8], around(away[NZ - 8 :])], axis=0)
        depth = (bump_of(away * scale) * row(5)).astype(jnp.bfloat16)
        plane = jnp.concatenate(
            [along_first * along_second[y : y + 1, :] for y in wanted], axis=0
        ).astype(jnp.bfloat16)
        total[...] += lax.dot_general(
            plane, depth, (((1,), (1,)), ((), ())), preferred_element_type=jnp.float32
        )
        return carry

    lax.fori_loop(0, SLABS // BLOCK, step, 0, unroll=2)


def rim_kernel(arrived, lower, upper, held, total):
    deposit_rows(arrived, held, total, [*range(GHOST), *range(GHOST + CY, WIDE)])
    lower[...] = total[: GHOST * EXT]
    upper[...] = total[GHOST * EXT :]


def inner_kernel(arrived, tables, inner, table, held, arrival):
    copy = pltpu.make_async_copy(tables.at[lax.axis_index("slab") % 8], table, arrival)
    copy.start()
    deposit_rows(arrived, held, inner, range(GHOST, GHOST + CY))
    copy.wait()


def join_kernel(inner, before, after, out):
    for y in range(CY):
        for group in range(GROUPS):
            value = inner[y * EXT + group * 8 : y * EXT + group * 8 + 8]
            if y < GHOST:
                at = y * EXT + group * 8
                value = value + before[at : at + 8]
            if y >= CY - GHOST:
                at = (y - CY + GHOST) * EXT + group * 8
                value = value + after[at : at + 8]
            out[y * 8 : y * 8 + 8, 0, group * LANES : (group + 1) * LANES] = value


def slab_kernel(table, value, out):
    for group in range(GROUPS - 1):
        rows = value[:, 0, group * LANES : (group + 1) * LANES]
        if group == 0:
            last = value[:, 0, (GROUPS - 1) * LANES :]
            rows = rows + jnp.concatenate([last[SLABS - 1 :], last[: SLABS - 1]], axis=0)
        result = jnp.dot(
            table[group], rows, precision=lax.Precision.HIGHEST, preferred_element_type=jnp.float32
        )
        out[:, group, :] = result[:SLABS]
        out[:, GROUPS - 1 + group, :] = result[SLABS:]


def plane_kernel(table, value, out, held, leaves):
    rows = jnp.concatenate(
        [value[y * 8 : y * 8 + 8].reshape(SLABS, LANES) for y in range(CY)], axis=1
    )
    copies = []
    for part in range(2):
        span = pl.ds(part * PLANES, PLANES)
        result = jnp.dot(
            table[span, :], rows, precision=lax.Precision.HIGHEST, preferred_element_type=jnp.float32
        )
        for y in range(CY):
            held[span, y, :] = result[:, y * LANES : (y + 1) * LANES]
        copies.append(pltpu.make_async_copy(held.at[span], out.at[span], leaves.at[part]))
        copies[part].start()
    for copy in copies:
        copy.wait()


def slab_tables():
    device = np.arange(SLABS)
    frequency = np.zeros(SLABS, np.int64)
    for bit in range(6):
        frequency += (device >> bit & 1) << 5 - bit
    offset = np.arange(8)[:, None] + 8 * np.arange(4)[None, :] - GHOST
    cell = PLANES * device[None, None, None, :] + offset[:, :, None, None]
    angle = 2.0 * np.pi * (frequency[None, None, :, None] * cell % NX) / NX
    table = np.concatenate([np.cos(angle), -np.sin(angle)], axis=2)
    return (table / math.sqrt(NX)).astype(np.float32)


def plane_table():
    offset = np.arange(8)[:, None] + 8 * np.arange(4)[None, :] - GHOST
    angle = 2.0 * np.pi * (np.arange(PLANES)[:, None, None] * offset[None] % PLANES) / PLANES
    real = np.stack([np.cos(angle), np.sin(angle)], axis=2)
    imag = np.stack([-np.sin(angle), np.cos(angle)], axis=2)
    return np.stack([real, imag]).reshape(2 * PLANES, 8 * 2 * 4).astype(np.float32)


def call(kernel, out, scratch=(), specs=None, leave=None, flops=0, moved=0):
    return pl.pallas_call(
        kernel,
        out_shape=out,
        **({} if specs is None else {"in_specs": specs}),
        **({} if leave is None else {"out_specs": leave}),
        scratch_shapes=list(scratch),
        compiler_params=pltpu.CompilerParams(vmem_limit_bytes=VMEM),
        cost_estimate=pl.CostEstimate(flops=flops, bytes_accessed=moved, transcendentals=0),
    )


def shape(*dims):
    return jax.ShapeDtypeStruct(dims, jnp.float32)


def bucket(live_counts, cell_x, cell_y, cell_z, offsets, radius_bin, masses, slab_dest):
    block = (ROWS, LANES)
    sources = [slab_dest.reshape(block), offsets] + [
        value.reshape(block) for value in (cell_x, cell_y, cell_z, radius_bin, masses)
    ]
    return call(
        bucket_kernel,
        shape(SLABS, 1, 5 * LANES),
        [pltpu.VMEM(value.shape, value.dtype) for value in sources]
        + [
            pltpu.VMEM((3, ROWS, LANES), jnp.float32),
            pltpu.VMEM((PIECES, ROWS, LANES), jnp.float32),
            pltpu.VMEM((ROWS * SLABS, LANES), jnp.bfloat16),
            pltpu.VMEM((ROWS * SLABS, 2 * LANES), jnp.float32),
            pltpu.SemaphoreType.DMA((7,)),
        ],
        [pl.BlockSpec(memory_space=pltpu.SMEM)] + [pl.BlockSpec(memory_space=pltpu.HBM)] * 7,
        flops=10**9,
        moved=10**6,
    )(live_counts, *[pltpu.with_memory_space_constraint(value, pltpu.HBM) for value in sources])


HELD = pltpu.VMEM((6, SLABS, LANES), jnp.float32)


def deposit_rims(arrived):
    rim = shape(GHOST * EXT, NZ)
    scratch = [HELD, pltpu.VMEM((2 * GHOST * EXT, NZ), jnp.float32)]
    return call(rim_kernel, (rim, rim), scratch, flops=5 * 10**8, moved=10**6)(arrived)


def deposit_inner(arrived):
    tables = pltpu.with_memory_space_constraint(jnp.asarray(slab_tables()), pltpu.HBM)
    return call(
        inner_kernel,
        (shape(CY * EXT, NZ), shape(*tables.shape[1:])),
        [HELD, pltpu.SemaphoreType.DMA],
        [pl.BlockSpec(memory_space=pltpu.VMEM), pl.BlockSpec(memory_space=pltpu.HBM)],
        flops=10**9,
        moved=10**6,
    )(arrived, tables)


def exchanged(value):
    return lax.all_to_all(value, "slab", split_axis=0, concat_axis=0, tiled=True)


def local(cell_x, cell_y, cell_z, offsets, radius_bin, masses, slab_dest, live_counts):
    outgoing = bucket(
        live_counts, cell_x, cell_y, cell_z, offsets, radius_bin, masses, slab_dest
    )
    arrived = exchanged(outgoing)
    lower, upper = deposit_rims(arrived)
    count = lax.axis_size("pencil")
    up = [(i, (i + 1) % count) for i in range(count)]
    before = lax.ppermute(upper, "pencil", up)
    after = lax.ppermute(lower, "pencil", [(j, i) for i, j in up])
    inner, table = deposit_inner(arrived)
    joined = call(join_kernel, shape(SLABS, 1, GROUPS * LANES))(inner, before, after)
    crossing = exchanged(joined)
    partial = call(slab_kernel, shape(SLABS, 2 * (GROUPS - 1), LANES))(table, crossing)
    back = exchanged(partial)
    final = call(
        plane_kernel,
        shape(2 * PLANES, CY, NZ),
        [pltpu.VMEM((2 * PLANES, CY, NZ), jnp.float32), pltpu.SemaphoreType.DMA((2,))],
        leave=pl.BlockSpec(memory_space=pltpu.HBM),
    )(jnp.asarray(plane_table()), back)
    return final.reshape(2, PLANES, CY, NZ)


def solution(mesh):
    in_specs = (
        P(("slab", "pencil")),
        P(("slab", "pencil")),
        P(("slab", "pencil")),
        P(None, ("slab", "pencil")),
        P(("slab", "pencil")),
        P(("slab", "pencil")),
        P(("slab", "pencil")),
        P(("slab", "pencil")),
    )
    out_specs = P(None, "slab", "pencil", None)
    return jax.shard_map(local, mesh=mesh, in_specs=in_specs, out_specs=out_specs, check_vma=False)
```
